512 devices in a mesh: seq: 128 (over z, y, core), tp: 4 (over x).
Axes of the slice: x: 4, y: 8, z: 8, core: 2. Of those that a mesh axis runs over, the one named last changes fastest.
Arguments:
- hidden_in: bfloat16 [32768, 4096], P('seq', 'tp'), may hold values from -6 to 6
- doc_lengths: int32 [64], replicated, may hold values from 1 to 1024, 32768 in all
- w_query: bfloat16 [4096, 4096], P(None, 'tp'), may hold values from -1 to 1
- w_key: bfloat16 [4096, 1024], P(None, 'tp'), may hold values from -1 to 1
- w_value: bfloat16 [4096, 1024], P(None, 'tp'), may hold values from -0.09375 to 0.09375
- w_out: bfloat16 [4096, 4096], P('tp'), may hold values from -0.09375 to 0.09375
Outputs:
- attn_out: bfloat16 [32768, 4096], P('seq', 'tp')
The draws below stay inside these ranges and needn't reach their ends.
Inputs may be any that keep to these rules, and one draw needn't show every extreme that they name: `doc_lengths`: every document has 1 to 1024 tokens, the longest exactly 1024, and the lengths sum to 32768.
All inputs are finite; a program needn't handle non-finite values.
Results may differ from the reference program's by a relative error of at most 0.02.
Values may be sent and summed in bfloat16 or wider, within the bound.
A program may use at most 128 MiB of HBM per device.

```python
import math
import jax
import jax.numpy as jnp
import numpy as np
from jax import lax

D = 4096
QH = 32
KVH = 8
HEAD_DIM = 128
TOK_DEV = 256
SPAN = 4
TOKENS = 32768
MOST_DOC = 1024
DOCS = 64
N_SEQ = 128
N_TP = 4


def projection_noise(key, heads):
    base = jnp.clip(jax.random.normal(key, (D, heads * HEAD_DIM), jnp.float32), -6.0, 6.0)
    return base * float(D) ** (-0.5)


def draw_hidden_in(key, part):
    key = jax.random.fold_in(key, 5)
    rows = jnp.clip(jax.random.normal(key, (TOKENS, D), jnp.float32), -6.0, 6.0)
    return rows.astype(jnp.bfloat16)


def draw_w_query(key, part):
    key = jax.random.fold_in(key, 3)
    matrix = projection_noise(key, QH)
    return matrix.astype(jnp.bfloat16)


def draw_w_key(key, part):
    key = jax.random.fold_in(key, 7)
    matrix = projection_noise(key, KVH)
    return matrix.astype(jnp.bfloat16)


def levels(key, shape, cuts, low, high):
    def one(dim, blocks):
        draws = jax.random.uniform(jax.random.fold_in(jax.random.fold_in(key, 6), dim), (blocks,), jnp.float32, low / len(cuts), high / len(cuts))
        return jnp.repeat(jnp.exp(draws), shape[dim] // blocks).reshape((-1,) + (1,) * (len(shape) - dim - 1))

    gain = one(*cuts[0])
    for cut in cuts[1:]:
        gain = gain * one(*cut)
    return gain


def profile(amount, total, most, slope):
    weights = [(1 << 20) // math.isqrt(grade ** slope) + 1 for grade in range(2, amount + 1)]
    surplus, counts = total - most - (amount - 1), [1] * (amount - 1)
    while surplus > 0:
        candidates = [i for i in range(amount - 1) if counts[i] < most]
        mass, remaining = sum([weights[i] for i in candidates]), surplus
        for i in candidates:
            extra = min(most - counts[i], max(1, remaining * weights[i] // mass), surplus)
            counts[i] = counts[i] + extra
            surplus = surplus - extra
    return np.array([most] + counts)


def uneven_parts(key, number_of, total, limit, lean):
    if number_of == 2:
        one = jax.random.randint(key, (), max(1, total - limit), min(limit, total - 1) + 1)
        return jnp.stack([one, total - one])
    tallies = jnp.asarray(profile(number_of, total, limit, lean), jnp.int32)
    twos = (number_of - 1) // 2
    donor, receiver = tallies[1:1 + 2 * twos:2], tallies[2:2 + 2 * twos:2]
    room = jnp.minimum(donor - 1, limit - receiver)
    moved = jax.random.randint(jax.random.fold_in(key, 1), (twos,), 0, 1 << 20) % (room + 1)
    tallies = tallies.at[1:1 + 2 * twos:2].set(donor - moved).at[2:2 + 2 * twos:2].set(receiver + moved)
    return tallies[jax.random.permutation(jax.random.fold_in(key, 2), number_of)]


def normal_values(own_key, extent, spread, bound, cuts=(), held_as=jnp.bfloat16):
    values = spread * jax.random.normal(own_key, extent, jnp.float32)
    if cuts:
        values = values * levels(own_key, extent, cuts, -0.22, 0.18)
    return jnp.clip(values, -bound, bound).astype(held_as)


def setup_inputs(seed: int = 0) -> dict:
    splits = jax.random.split(jax.random.key(seed), 7)
    return {
        "hidden_in": draw_hidden_in(jax.random.fold_in(splits[6], 71), 0),
        "doc_lengths": uneven_parts(splits[1], DOCS, TOKENS, MOST_DOC, 2).astype(jnp.int32),
        "w_query": draw_w_query(jax.random.fold_in(splits[6], 71), 0),
        "w_key": draw_w_key(jax.random.fold_in(splits[6], 71), 0),
        "w_value": normal_values(splits[4], (D, KVH * HEAD_DIM), D ** -0.5, 0.09375, ((1, 4),)),
        "w_out": normal_values(splits[5], (QH * HEAD_DIM, D), (QH * HEAD_DIM) ** -0.5, 0.09375, ((0, 4),)),
    }


def inverse_frequencies(head_dim):
    exponent = jnp.arange(0, head_dim, 2, dtype=jnp.float32) / head_dim
    base_freq = jnp.power(jnp.float32(500000.0), -exponent)
    wavelength = 2.0 * math.pi / base_freq
    smooth_part = (8192.0 / wavelength - 1.0) / 3.0
    blended = (1.0 - smooth_part) * base_freq / 8.0 + smooth_part * base_freq
    return jnp.where(wavelength < 2048.0, base_freq, jnp.where(wavelength > 8192.0, base_freq / 8.0, blended))

def rotary_embed(head_values, positions):
    head_dim = head_values.shape[-1]
    half_dim = head_dim // 2
    frequencies = inverse_frequencies(head_dim)
    angles = positions.astype(jnp.float32)[:, None] * frequencies[None, :]
    cosine = jnp.cos(angles)[:, None, :]
    sine_part = jnp.sin(angles)[:, None, :]
    front_half = head_values[..., :half_dim]
    back_half = head_values[..., half_dim:]
    return jnp.concatenate([front_half * cosine - back_half * sine_part, back_half * cosine + front_half * sine_part], axis=-1)

def document_starts(doc_lengths, positions):
    document_ends = jnp.cumsum(doc_lengths).astype(jnp.int32)
    picked = jnp.where(document_ends[None, :] <= positions[:, None], doc_lengths[None, :], 0)
    return lax.optimization_barrier(jnp.sum(picked, axis=1)).astype(jnp.int32)

def reference(hidden_in, doc_lengths, w_query, w_key, w_value, w_out):
    positions = jnp.arange(TOKENS, dtype=jnp.int32)
    starts = document_starts(doc_lengths, positions)
    within = positions - starts
    group = QH // KVH
    queries = rotary_embed(jnp.dot(hidden_in, w_query, preferred_element_type=jnp.float32).reshape(TOKENS, QH, HEAD_DIM), within).astype(jnp.bfloat16)
    keys = rotary_embed(jnp.dot(hidden_in, w_key, preferred_element_type=jnp.float32).reshape(TOKENS, KVH, HEAD_DIM), within).astype(jnp.bfloat16)
    values_all = jnp.dot(hidden_in, w_value, preferred_element_type=jnp.float32).astype(jnp.bfloat16).reshape(TOKENS, KVH, HEAD_DIM)
    reach = SPAN * TOK_DEV
    padded_keys = jnp.concatenate([jnp.zeros((reach, KVH, HEAD_DIM), jnp.bfloat16), keys], axis=0)
    padded_values = jnp.concatenate([jnp.zeros((reach, KVH, HEAD_DIM), jnp.bfloat16), values_all], axis=0)
    score_scale = 1.0 / math.sqrt(HEAD_DIM)

    def one_block(block_index):
        first_query = (block_index * TOK_DEV).astype(jnp.int32)
        block_queries = lax.dynamic_slice_in_dim(queries, first_query, TOK_DEV, 0).reshape(TOK_DEV, KVH, group, HEAD_DIM).astype(jnp.float32)
        block_keys = lax.dynamic_slice_in_dim(padded_keys, first_query, reach + TOK_DEV, 0).astype(jnp.float32)
        block_values = lax.dynamic_slice_in_dim(padded_values, first_query, reach + TOK_DEV, 0).astype(jnp.float32)
        query_pos = first_query + jnp.arange(TOK_DEV, dtype=jnp.int32)
        key_pos = first_query - reach + jnp.arange(reach + TOK_DEV, dtype=jnp.int32)
        query_start = lax.dynamic_slice_in_dim(starts, first_query, TOK_DEV, 0)
        visible = (key_pos[None, :] >= query_start[:, None]) & (key_pos[None, :] <= query_pos[:, None])
        scores = jnp.einsum('qgrd,kgd->grqk', block_queries, block_keys) * score_scale
        scores = jnp.where(visible, scores, -1e+30)
        peak = lax.optimization_barrier(jnp.max(scores, axis=-1, keepdims=True))
        weights = jnp.where(visible, jnp.exp(scores - peak), 0.0)
        probs = (weights / lax.optimization_barrier(jnp.sum(weights, axis=-1, keepdims=True))).astype(jnp.bfloat16)
        context = jnp.einsum('grqk,kgd->qgrd', probs.astype(jnp.float32), block_values)
        return context.reshape(TOK_DEV, QH * HEAD_DIM).astype(jnp.bfloat16)
    context_all = lax.map(one_block, jnp.arange(N_SEQ, dtype=jnp.int32)).reshape(TOKENS, QH * HEAD_DIM)
    width_part = QH * HEAD_DIM // N_TP
    total = jnp.zeros((TOKENS, D), jnp.float32)
    for part_index in range(N_TP):
        partial_value = jnp.dot(context_all[:, part_index * width_part:(part_index + 1) * width_part], w_out[part_index * width_part:(part_index + 1) * width_part, :], preferred_element_type=jnp.float32).astype(jnp.bfloat16)
        partial_value = lax.optimization_barrier(partial_value)
        total = total + partial_value.astype(jnp.float32)
    return total.astype(jnp.bfloat16)
```

```python
import functools
import math

import jax
import jax.numpy as jnp
import numpy as np
from jax import lax
from jax.experimental import pallas as pl
from jax.experimental.pallas import tpu as pltpu
from jax.sharding import PartitionSpec as P

HEAD = 128
CHUNKS = 4
REACH = 4
MESH = pl.DeviceIdType.MESH
F32 = jnp.float32
BF16 = jnp.bfloat16


def inverse_frequencies():
    exponent = np.arange(0, HEAD, 2, dtype=np.float32) / np.float32(HEAD)
    base = np.power(np.float32(500000.0), -exponent).astype(np.float32)
    wavelength = (2.0 * math.pi / base).astype(np.float32)
    smooth = (8192.0 / wavelength - 1.0) / 3.0
    blended = (1.0 - smooth) * base / 8.0 + smooth * base
    freq = np.where(wavelength < 2048.0, base, np.where(wavelength > 8192.0, base / 8.0, blended))
    return np.concatenate([freq, freq]).astype(np.float32)[None, :]


def layer(
    n_seq, n_tp,
    len_ref, freq_ref, hid_hbm, wq_hbm, wk_hbm, wv_hbm, wo_hbm, out_hbm,
    hid, w, wo, acc, kv, q, tab, bias, ctx,
    far_s, right_p, left_p, own_p, right_s, left_s, half_l, half_r, full_l, full_r, out_v,
    w_sem, hid_sem, near_s, near_r, fwd_s, fwd_r, kv_s, kv_r, rs_s, rs_r, out_sem,
):
    tok, dx = hid_hbm.shape
    docs = len_ref.shape[0]
    rows = tok // CHUNKS
    nkv = 2 * HEAD
    nq = wq_hbm.shape[1]
    heads = nq // HEAD
    group = heads // 2
    half = dx // 2
    seq = lax.axis_index("seq")
    x = lax.axis_index("tp")
    core = lax.rem(seq, 2)
    right = {"tp": lax.rem(x + 1, n_tp)}
    left = {"tp": lax.rem(x + n_tp - 1, n_tp)}
    ahead = {"seq": lax.rem(seq + 2, n_seq)}
    behind = {"seq": lax.rem(seq + n_seq - 2, n_seq)}
    sibling = {"seq": seq + 1 - 2 * core}

    loads = []
    shards = (x, lax.rem(x + n_tp - 1, n_tp), lax.rem(x + 1, n_tp), lax.rem(x + 2, n_tp))
    own_copy = pltpu.make_async_copy(hid_hbm, hid.at[:, pl.ds(0, dx)], hid_sem)
    own_copy.start()
    for r in range(4):
        src = pl.ds(pl.multiple_of(shards[r] * dx, dx), dx)
        dst = pl.ds(r * dx, dx)
        for k, (ref, at, width) in enumerate(
            ((wk_hbm, 0, nkv), (wv_hbm, nkv, nkv), (wq_hbm, 2 * nkv, nq))
        ):
            copy = pltpu.make_async_copy(
                ref.at[src], w.at[dst, pl.ds(at, width)], w_sem.at[3 * r + k]
            )
            copy.start()
            loads.append(copy)
    out_loads = []
    for r, shard in enumerate((shards[0], shards[2], shards[1], shards[3])):
        columns = pl.ds(pl.multiple_of(shard * dx, dx), dx)
        copy = pltpu.make_async_copy(wo_hbm.at[:, columns], wo.at[r], w_sem.at[12 + r])
        copy.start()
        out_loads.append(copy)

    barrier = pltpu.get_barrier_semaphore()
    for other in (right, left, ahead, behind, sibling):
        pl.semaphore_signal(barrier, inc=1, device_id=other, device_id_type=MESH)
    pl.semaphore_wait(barrier, 5)

    def remote(src, dst, send, recv, to):
        return pltpu.make_async_remote_copy(
            src_ref=src, dst_ref=dst, send_sem=send, recv_sem=recv,
            device_id=to, device_id_type=MESH,
        )

    def chunk(c, base=0):
        return pl.ds(base + c * rows, rows)

    def near(c):
        return (
            remote(hid_hbm.at[chunk(c)], hid.at[chunk(c), pl.ds(dx, dx)],
                   near_s.at[0, c], near_r.at[0, c], right),
            remote(hid_hbm.at[chunk(c)], hid.at[chunk(c), pl.ds(2 * dx, dx)],
                   near_s.at[1, c], near_r.at[1, c], left),
        )

    def forward(c):
        return (
            remote(hid.at[chunk(c), pl.ds(dx, half)], hid.at[chunk(c), pl.ds(3 * dx, half)],
                   fwd_s.at[0, c], fwd_r.at[0, c], right),
            remote(hid.at[chunk(c), pl.ds(2 * dx + half, half)],
                   hid.at[chunk(c), pl.ds(3 * dx + half, half)],
                   fwd_s.at[1, c], fwd_r.at[1, c], left),
        )

    def kv_rows(place, c):
        return kv.at[:, pl.ds(pl.multiple_of((place + core) * tok + c * rows, rows), rows),
                     pl.ds(0, nkv)]

    def kv_copy(kind, c):
        src, dst, to = (
            (4, 2, ahead), (2, 0, ahead), (4, 4, sibling), (2, 2, sibling), (0, 0, sibling)
        )[kind]
        return remote(kv_rows(src, c), kv_rows(dst, c), kv_s.at[kind, c], kv_r.at[kind, c], to)

    started = []

    def start(copies):
        for copy in copies:
            copy.start()
            started.append(copy)

    nears = [near(c) for c in range(CHUNKS)]
    forwards = [forward(c) for c in range(CHUNKS)]
    kvs = [[kv_copy(kind, c) for c in range(CHUNKS)] for kind in range(5)]
    start(nears[0])
    start(nears[1])

    row = lax.broadcasted_iota(jnp.int32, (tok, HEAD), 0)
    lane = lax.broadcasted_iota(jnp.int32, (tok, HEAD), 1)
    pos = row + seq * tok

    def next_doc(d, state):
        end, first = state
        end = end + len_ref[d]
        return end, jnp.where(pos >= end, end, first)

    _, first = lax.fori_loop(0, docs, next_doc, (jnp.int32(0), jnp.zeros_like(pos)))
    angle = (pos - first).astype(F32) * freq_ref[...]
    cosine = jnp.cos(angle)
    sine = jnp.where(lane < HEAD // 2, -1.0, 1.0) * jnp.sin(angle)
    scale = math.log2(math.e) / math.sqrt(HEAD)
    tab[0] = cosine
    tab[1] = sine
    tab[2] = cosine * scale
    tab[3] = sine * scale
    low = first - (seq * tok - REACH * tok)
    high = row + REACH * tok
    span = bias.shape[1]
    step = 2 * rows
    for b in range(tok // step):
        part = slice(b * step, (b + 1) * step)
        for k in range(span // HEAD):
            key = lane[part] + (b * step + k * HEAD)
            seen = (key >= low[part]) & (key <= high[part])
            bias[part, k * HEAD:(k + 1) * HEAD] = jnp.where(seen, 0.0, -1e30)
    kv[:, :, nkv:] = jnp.ones((2, kv.shape[1], HEAD), BF16)

    tile = 2 * HEAD
    tiles = w.shape[1] // tile

    def project_near(c):
        @pl.loop(0, tiles)
        def _(j):
            at = pl.ds(pl.multiple_of(j * tile, tile), tile)
            acc[chunk(c), at] = jnp.dot(
                hid[chunk(c), 0:3 * dx], w[0:3 * dx, at], preferred_element_type=F32
            )

    def far_tile(c, at):
        return acc[chunk(c), at] + jnp.dot(
            hid[chunk(c), 3 * dx:], w[3 * dx:, at], preferred_element_type=F32
        )

    def rotated(part, c, cos_at):
        return part * tab[cos_at, chunk(c)] + pltpu.roll(part, HEAD // 2, 1) * tab[cos_at + 1, chunk(c)]

    def project_far(c):
        own = pl.ds(pl.multiple_of((4 + core) * tok + c * rows, rows), rows)
        keys = far_tile(c, pl.ds(0, tile))
        values = far_tile(c, pl.ds(tile, tile))
        for g in range(2):
            part = slice(g * HEAD, (g + 1) * HEAD)
            kv[g, own, 0:HEAD] = rotated(keys[:, part], c, 0).astype(BF16)
            kv[g, own, HEAD:nkv] = values[:, part].astype(BF16)
        start([kvs[0][c], kvs[2][c]])

        @pl.loop(0, tiles - 2)
        def _(j):
            two = far_tile(c, pl.ds(pl.multiple_of((j + 2) * tile, tile), tile))
            for k in range(2):
                head = 2 * j + k
                place = pl.ds(pl.multiple_of(lax.rem(head, group) * rows, rows), rows)
                q[head // group, c, place] = rotated(
                    two[:, k * HEAD:(k + 1) * HEAD], c, 2
                ).astype(BF16)

    def pass_on(c):
        kvs[0][c].wait_recv()
        start([kvs[1][c], kvs[3][c]])

    def pass_far(c):
        kvs[1][c].wait_recv()
        start([kvs[4][c]])

    own_copy.wait()
    for c in range(CHUNKS):
        for copy in nears[c]:
            copy.wait_recv()
        start(forwards[c])
        if c + 2 < CHUNKS:
            start(nears[c + 2])
        if c == 0:
            for copy in loads[:9]:
                copy.wait()
        project_near(c)
        if c >= 1:
            if c == 1:
                for copy in loads[9:]:
                    copy.wait()
            for copy in forwards[c - 1]:
                copy.wait_recv()
            project_far(c - 1)
        if c >= 2:
            pass_on(c - 2)
        if c >= 3:
            pass_far(c - 3)
    for copy in forwards[CHUNKS - 1]:
        copy.wait_recv()
    project_far(CHUNKS - 1)
    pass_on(CHUNKS - 2)
    pass_far(CHUNKS - 3)
    pass_on(CHUNKS - 1)
    pass_far(CHUNKS - 2)
    pass_far(CHUNKS - 1)
    for kind in (2, 3, 4):
        for c in range(CHUNKS):
            kvs[kind][c].wait_recv()
    for copy in out_loads:
        copy.wait()

    def attend(c):
        first_key = (c // 2) * step
        window = pl.ds(pl.multiple_of(core * tok + first_key, step), span)
        for g in range(2):
            scores = lax.dot_general(
                q[g, c], kv[g, window, 0:HEAD], (((1,), (1,)), ((), ())),
                preferred_element_type=F32,
            )
            scores = scores.reshape(group, rows, span) + bias[chunk(c)][None]
            peak = jnp.max(scores, axis=2, keepdims=True)
            weights = jnp.exp2(scores - peak).reshape(group * rows, span).astype(BF16)
            both = jnp.dot(weights, kv[g, window, HEAD:], preferred_element_type=F32)
            value = (both[:, 0:HEAD] / both[:, HEAD:]).astype(BF16)
            for h in range(group):
                at = (g * group + h) * HEAD
                ctx[c, :, at:at + HEAD] = value[h * rows:(h + 1) * rows]

    out_tile = min(512, dx)

    def output_part(c, r, ref):
        @pl.loop(0, dx // out_tile)
        def _(j):
            at = pl.ds(pl.multiple_of(j * out_tile, out_tile), out_tile)
            ref[c, :, at] = jnp.dot(ctx[c], wo[r, :, at], preferred_element_type=F32).astype(
                ref.dtype
            )

    far_copies = [
        (
            remote(far_s.at[c, :, pl.ds(0, half)], half_l.at[c], rs_s.at[0, c], rs_r.at[0, c], right),
            remote(far_s.at[c, :, pl.ds(half, half)], half_r.at[c], rs_s.at[1, c], rs_r.at[1, c], left),
        )
        for c in range(CHUNKS)
    ]
    sum_copies = [
        (
            remote(right_s.at[c], full_l.at[c], rs_s.at[2, c], rs_r.at[2, c], right),
            remote(left_s.at[c], full_r.at[c], rs_s.at[3, c], rs_r.at[3, c], left),
        )
        for c in range(CHUNKS)
    ]

    def add_halves(c):
        far_copies[c][0].wait_recv()
        right_s[c, :, 0:half] = (right_p[c, :, 0:half] + half_l[c].astype(F32)).astype(BF16)
        right_s[c, :, half:] = right_p[c, :, half:].astype(BF16)
        start(sum_copies[c][:1])
        far_copies[c][1].wait_recv()
        left_s[c, :, 0:half] = left_p[c, :, 0:half].astype(BF16)
        left_s[c, :, half:] = (left_p[c, :, half:] + half_r[c].astype(F32)).astype(BF16)
        start(sum_copies[c][1:])

    out_copies = []

    def finish(c):
        for copy in sum_copies[c]:
            copy.wait_recv()
        out_v[c] = (own_p[c] + (full_l[c].astype(F32) + full_r[c].astype(F32))).astype(BF16)
        copy = pltpu.make_async_copy(out_v.at[c], out_hbm.at[chunk(c)], out_sem.at[c])
        copy.start()
        out_copies.append(copy)

    for c in range(CHUNKS):
        attend(c)
        output_part(c, 3, far_s)
        start(far_copies[c])
        if c >= 1:
            add_halves(c - 1)
        output_part(c, 1, right_p)
        output_part(c, 2, left_p)
        output_part(c, 0, own_p)
        if c >= 2:
            finish(c - 2)
    add_halves(CHUNKS - 1)
    finish(CHUNKS - 2)
    finish(CHUNKS - 1)
    for copy in started:
        copy.wait_send()
    for copy in out_copies:
        copy.wait()


def body(n_seq, n_tp, hidden_in, doc_lengths, w_query, w_key, w_value, w_out):
    tok, dx = hidden_in.shape
    rows = tok // CHUNKS
    nq = w_query.shape[1]
    wide = w_key.shape[1] + w_value.shape[1] + nq
    span = REACH * tok + 2 * rows
    group = nq // HEAD // 2
    anywhere = pl.BlockSpec(memory_space=pl.ANY)
    dma = pltpu.SemaphoreType.DMA
    part = (CHUNKS, rows, dx)
    return pl.pallas_call(
        functools.partial(layer, n_seq, n_tp),
        out_shape=jax.ShapeDtypeStruct((tok, dx), BF16),
        in_specs=[pl.BlockSpec(memory_space=pltpu.SMEM), pl.BlockSpec(memory_space=pltpu.VMEM)]
        + [anywhere] * 5,
        out_specs=anywhere,
        scratch_shapes=[
            pltpu.VMEM((tok, 4 * dx), BF16),
            pltpu.VMEM((4 * dx, wide), BF16),
            pltpu.VMEM((4, nq, dx), BF16),
            pltpu.VMEM((tok, wide), F32),
            pltpu.VMEM((2, 6 * tok, 3 * HEAD), BF16),
            pltpu.VMEM((2, CHUNKS, group * rows, HEAD), BF16),
            pltpu.VMEM((4, tok, HEAD), F32),
            pltpu.VMEM((tok, span), F32),
            pltpu.VMEM((CHUNKS, rows, nq), BF16),
            pltpu.VMEM(part, BF16),
            pltpu.VMEM(part, F32),
            pltpu.VMEM(part, F32),
            pltpu.VMEM(part, F32),
            pltpu.VMEM(part, BF16),
            pltpu.VMEM(part, BF16),
            pltpu.VMEM((CHUNKS, rows, dx // 2), BF16),
            pltpu.VMEM((CHUNKS, rows, dx // 2), BF16),
            pltpu.VMEM(part, BF16),
            pltpu.VMEM(part, BF16),
            pltpu.VMEM(part, BF16),
            dma((16,)),
            dma(()),
            dma((2, CHUNKS)),
            dma((2, CHUNKS)),
            dma((2, CHUNKS)),
            dma((2, CHUNKS)),
            dma((5, CHUNKS)),
            dma((5, CHUNKS)),
            dma((4, CHUNKS)),
            dma((4, CHUNKS)),
            dma((CHUNKS,)),
        ],
        compiler_params=pltpu.CompilerParams(
            collective_id=0, has_side_effects=True, vmem_limit_bytes=58 * 2**20
        ),
        cost_estimate=pl.CostEstimate(
            flops=7 * 10**9, bytes_accessed=22 * 10**6, transcendentals=2 * 10**6
        ),
        name="layer",
    )(doc_lengths, jnp.asarray(inverse_frequencies()), hidden_in, w_query, w_key, w_value, w_out)


def solution(mesh):
    return jax.shard_map(
        functools.partial(body, mesh.shape["seq"], mesh.shape["tp"]),
        mesh=mesh,
        in_specs=(P("seq", "tp"), P(), P(None, "tp"), P(None, "tp"), P(None, "tp"), P("tp", None)),
        out_specs=P("seq", "tp"),
        check_vma=False,
    )
```

```python
import functools
import math

import jax
import jax.numpy as jnp
import numpy as np
from jax import lax
from jax.experimental import pallas as pl
from jax.experimental.pallas import tpu as pltpu
from jax.sharding import PartitionSpec as P

HEAD = 128
REACH = 4
GATHER = ((64, False, "pass"), (64, False, "pass"), (64, False, "pass"), (64, False, "two"))
SCATTER = ((64, False), (64, False), (64, False), (64, False))
SPAN = 1152
EARLY = 2
MESH = pl.DeviceIdType.MESH
F32 = jnp.float32
BF16 = jnp.bfloat16
OFF = frozenset()


def inverse_frequencies():
    exponent = np.arange(0, HEAD, 2, dtype=np.float32) / np.float32(HEAD)
    base = np.power(np.float32(500000.0), -exponent).astype(np.float32)
    wavelength = (2.0 * math.pi / base).astype(np.float32)
    smooth = (8192.0 / wavelength - 1.0) / 3.0
    blended = (1.0 - smooth) * base / 8.0 + smooth * base
    freq = np.where(wavelength < 2048.0, base, np.where(wavelength > 8192.0, base / 8.0, blended))
    return np.concatenate([freq, freq]).astype(np.float32)[None, :]


def bounds(chunks):
    at, out = 0, []
    for size in chunks:
        out.append((at, size))
        at += size
    return out


class Move:
    def __init__(self, copy, sends=None, lands=None):
        self.copy, self.sends, self.lands = copy, sends, lands

    @staticmethod
    def on(condition, act):
        if condition is None:
            act()
        else:
            pl.when(condition)(act)

    def start(self):
        self.on(self.sends, self.copy.start)

    def sent(self):
        self.on(self.sends, self.copy.wait_send)

    def landed(self):
        self.on(self.lands, self.copy.wait_recv)


class Nothing:
    def start(self):
        pass

    sent = landed = start


def layer(
    n_seq, n_tp,
    len_ref, freq_ref, hid_hbm, wq_hbm, wk_hbm, wv_hbm, wo_hbm, out_v,
    hid, w, wo, acc, kv, q, tab, bias, ctx,
    far_s, right_p, left_p, own_p, right_s, left_s, half_l, half_r, full_l, full_r, full_o,
    w_sem, hid_sem, near_s, near_r, fwd_s, fwd_r, kv_s, kv_r, rs_s, rs_r,
):
    tok, dx = hid_hbm.shape
    docs = len_ref.shape[0]
    nkv = 2 * HEAD
    nq = wq_hbm.shape[1]
    group = nq // HEAD // 2
    half = dx // 2
    seq = lax.axis_index("seq")
    x = lax.axis_index("tp")
    core = lax.rem(seq, 2)
    right = {"tp": lax.rem(x + 1, n_tp)}
    left = {"tp": lax.rem(x + n_tp - 1, n_tp)}
    across = {"tp": lax.rem(x + 2, n_tp)}
    sibling = {"seq": seq + 1 - 2 * core}
    ahead, ahead2, behind, behind2 = ({"seq": seq + d} for d in (2, 4, -2, -4))
    has_ahead, has_ahead2 = seq + 2 < n_seq, seq + 4 < n_seq
    has_behind, has_behind2 = seq >= 2, seq >= 4
    gather = bounds([c[0] for c in GATHER])
    scatter = bounds([c[0] for c in SCATTER])

    @pl.when(seq < 4)
    def _():
        kv[:, 0:4 * tok] = jnp.zeros((2, 4 * tok, 3 * HEAD), BF16)

    @pl.when(core == 0)
    def _():
        kv[:, 5 * tok:6 * tok, 0:nkv] = jnp.zeros((2, tok, nkv), BF16)

    barrier = pltpu.get_barrier_semaphore()

    def greet(other):
        pl.semaphore_signal(barrier, inc=1, device_id=other, device_id_type=MESH)

    for other in (right, left, across, sibling):
        greet(other)
    for other, there in (
        (ahead, has_ahead), (behind, has_behind), (ahead2, has_ahead2), (behind2, has_behind2)
    ):
        pl.when(there)(functools.partial(greet, other))

    shards = (x, lax.rem(x + n_tp - 1, n_tp), lax.rem(x + 1, n_tp), lax.rem(x + 2, n_tp))
    own_copy = pltpu.make_async_copy(hid_hbm, hid.at[:, pl.ds(0, dx)], hid_sem)
    own_copy.start()
    loads = {}

    def load(name, index, src, dst):
        copy = pltpu.make_async_copy(src, dst, w_sem.at[index])
        copy.start()
        loads.setdefault(name, []).append(copy)

    def load_keys(r):
        src = pl.ds(pl.multiple_of(shards[r] * dx, dx), dx)
        dst = pl.ds(r * dx, dx)
        name = "far" if r == 3 else "near"
        load(name, 3 * r, wk_hbm.at[src], w.at[dst, pl.ds(0, nkv)])
        load(name, 3 * r + 1, wv_hbm.at[src], w.at[dst, pl.ds(nkv, nkv)])

    load_keys(0)
    row = lax.broadcasted_iota(jnp.int32, (tok, HEAD), 0)
    lane = lax.broadcasted_iota(jnp.int32, (tok, HEAD), 1)
    pos = row + seq * tok

    def next_doc(d, state):
        end, first = state
        end = end + len_ref[d]
        return end, jnp.where(pos >= end, end, first)

    _, first = lax.fori_loop(0, docs, next_doc, (jnp.int32(0), jnp.zeros_like(pos)))
    angle = (pos - first).astype(F32) * freq_ref[...]
    cosine = jnp.cos(angle)
    sine = jnp.where(lane < HEAD // 2, -1.0, 1.0) * jnp.sin(angle)
    scale = math.log2(math.e) / math.sqrt(HEAD)
    tab[0] = cosine
    tab[1] = sine
    tab[2] = cosine * scale
    tab[3] = sine * scale
    low = first - (seq * tok - REACH * tok)
    high = row + REACH * tok
    for at, size in scatter:
        part = slice(at, at + size)
        for k in range(SPAN // HEAD):
            key = lane[part] + (at + k * HEAD)
            seen = (key >= low[part]) & (key <= high[part])
            bias[part, k * HEAD:(k + 1) * HEAD] = jnp.where(seen, 0.0, -1e30)
    kv[:, :, nkv:] = jnp.ones((2, kv.shape[1], HEAD), BF16)
    kv[:, 6 * tok:, 0:nkv] = jnp.zeros((2, kv.shape[1] - 6 * tok, nkv), BF16)

    others = 4
    for there in (has_ahead, has_behind, has_ahead2, has_behind2):
        others = others + jnp.where(there, 1, 0)
    pl.semaphore_wait(barrier, others)

    def remote(src, dst, send, recv, to, sends=None, lands=None, kind=""):
        if kind in OFF:
            return Nothing()
        copy = pltpu.make_async_remote_copy(
            src_ref=src, dst_ref=dst, send_sem=send, recv_sem=recv,
            device_id=to, device_id_type=MESH,
        )
        return Move(copy, sends, lands)

    def near(c):
        at = pl.ds(*gather[c])
        moves = [
            remote(hid_hbm.at[at], hid.at[at, pl.ds(dx, dx)],
                   near_s.at[0, c], near_r.at[0, c], right, kind="ag"),
            remote(hid_hbm.at[at], hid.at[at, pl.ds(2 * dx, dx)],
                   near_s.at[1, c], near_r.at[1, c], left, kind="ag"),
        ]
        return moves

    def far(c):
        at = pl.ds(*gather[c])
        if GATHER[c][1]:
            return [remote(hid_hbm.at[at], hid.at[at, pl.ds(3 * dx, dx)],
                           fwd_s.at[0, c], fwd_r.at[0, c], across, kind="ag")]
        return [
            remote(hid.at[at, pl.ds(dx, half)], hid.at[at, pl.ds(3 * dx, half)],
                   fwd_s.at[0, c], fwd_r.at[0, c], right, kind="ag"),
            remote(hid.at[at, pl.ds(2 * dx + half, half)],
                   hid.at[at, pl.ds(3 * dx + half, half)],
                   fwd_s.at[1, c], fwd_r.at[1, c], left, kind="ag"),
        ]

    def place(block, c):
        first, size = gather[c]
        return pl.ds(pl.multiple_of((block + core) * tok + first, 16), size)

    def kv_move(kind, c):
        passes = GATHER[c][2] == "pass"
        first_core, second_core = core == 0, core == 1
        src, dst, to, sends, lands = (
            (4, 2, ahead, has_ahead, has_behind),
            (2, 0, ahead, has_ahead & has_behind, has_behind2) if passes
            else (4, 0, ahead2, has_ahead2, has_behind2),
            (4, 4, sibling, first_core, second_core),
            (2, 2, sibling, has_behind, has_behind),
            (0, 0, sibling, has_behind2 & second_core, has_behind2 & first_core),
        )[kind]
        return remote(
            kv.at[:, place(src, c), pl.ds(0, nkv)], kv.at[:, place(dst, c), pl.ds(0, nkv)],
            kv_s.at[kind, c], kv_r.at[kind, c], to, sends, lands, kind="kvx",
        )

    started = []

    def start(moves):
        for move in moves:
            move.start()
            started.append(move)

    def landed(moves):
        for move in moves:
            move.landed()

    count = len(GATHER)
    nears = [near(c) for c in range(count)]
    fars = [far(c) for c in range(count)]
    kvs = [[kv_move(kind, c) for c in range(count)] for kind in range(5)]
    def start_near(c):
        start(nears[c])
        if GATHER[c][1]:
            start(fars[c])

    for c in range(min(EARLY, count)):
        start_near(c)
    for r in (1, 2, 3):
        load_keys(r)
    for r in range(4):
        src = pl.ds(pl.multiple_of(shards[r] * dx, dx), dx)
        load("q", 3 * r + 2, wq_hbm.at[src], w.at[pl.ds(r * dx, dx), pl.ds(2 * nkv, nq)])
    for r, shard in enumerate((shards[0], shards[2], shards[1], shards[3])):
        columns = pl.ds(pl.multiple_of(shard * dx, dx), dx)
        load("out", 12 + r, wo_hbm.at[:, columns], wo.at[r])

    def near_keys(c):
        if "qkv" in OFF:
            return
        at = pl.ds(*gather[c])
        acc[at] = jnp.dot(hid[at, 0:3 * dx], w[0:3 * dx, 0:2 * nkv], preferred_element_type=F32)

    def rotated(part, at, which):
        return part * tab[which, at] + pltpu.roll(part, HEAD // 2, 1) * tab[which + 1, at]

    def far_keys(c):
        at = pl.ds(*gather[c])
        own = place(4, c)
        if "qkv" not in OFF:
            both = acc[at] + jnp.dot(
                hid[at, 3 * dx:], w[3 * dx:, 0:2 * nkv], preferred_element_type=F32
            )
            for g in range(2):
                one = slice(g * HEAD, (g + 1) * HEAD)
                kv[g, own, 0:HEAD] = rotated(both[:, one], at, 0).astype(BF16)
                kv[g, own, HEAD:nkv] = both[:, nkv + g * HEAD:nkv + (g + 1) * HEAD].astype(BF16)
        start([kvs[0][c], kvs[2][c]])
        if GATHER[c][2] == "two":
            start([kvs[1][c]])

    def pass_on(c):
        landed([kvs[0][c]])
        if GATHER[c][2] == "pass":
            start([kvs[1][c]])
        start([kvs[3][c]])

    def pass_far(c):
        landed([kvs[1][c]])
        start([kvs[4][c]])

    def project_queries(j):
        if "qkv" in OFF:
            return
        at = pl.ds(0, tok)
        two = jnp.dot(
            hid[...], w[:, 2 * nkv + 2 * j * HEAD:2 * nkv + 2 * (j + 1) * HEAD],
            preferred_element_type=F32,
        )
        for k in range(2):
            q[2 * j + k] = rotated(two[:, k * HEAD:(k + 1) * HEAD], at, 2).astype(BF16)

    def loaded(name):
        for copy in loads[name]:
            copy.wait()

    own_copy.wait()
    for c in range(count):
        landed(nears[c])
        if not GATHER[c][1]:
            start(fars[c])
        if c + EARLY < count:
            start_near(c + EARLY)
        if c == 0:
            loaded("near")
        near_keys(c)
        if c >= 1:
            if c == 1:
                loaded("far")
            landed(fars[c - 1])
            far_keys(c - 1)
        if c >= 2:
            pass_on(c - 2)
        if c >= 3:
            pass_far(c - 3)
    landed(fars[count - 1])
    far_keys(count - 1)
    loaded("q")
    pass_on(count - 2)
    pass_far(count - 3)
    project_queries(0)
    project_queries(1)
    pass_far(count - 2)
    project_queries(2)
    pass_on(count - 1)
    project_queries(3)
    pass_far(count - 1)
    loaded("out")
    for kind in (2, 3, 4):
        landed(kvs[kind])

    def attend(c):
        if "att" in OFF:
            return
        first, size = scatter[c]
        at = pl.ds(first, size)
        window = pl.ds(pl.multiple_of(core * tok + first, 16), SPAN)
        for g in range(2):
            mine = q[g * group:(g + 1) * group, at].reshape(group * size, HEAD)
            scores = lax.dot_general(
                mine, kv[g, window, 0:HEAD], (((1,), (1,)), ((), ())), preferred_element_type=F32
            )
            scores = scores.reshape(group, size, SPAN) + bias[at][None]
            peak = jnp.max(scores, axis=2, keepdims=True)
            weights = jnp.exp2(scores - peak).reshape(group * size, SPAN).astype(BF16)
            both = jnp.dot(weights, kv[g, window, HEAD:], preferred_element_type=F32)
            value = (both[:, 0:HEAD] / both[:, HEAD:]).astype(BF16)
            for h in range(group):
                to = (g * group + h) * HEAD
                ctx[at, to:to + HEAD] = value[h * size:(h + 1) * size]

    def output_part(c, r, ref):
        if "proj" in OFF:
            return
        at = pl.ds(*scatter[c])
        ref[at] = jnp.dot(ctx[at], wo[r], preferred_element_type=F32).astype(ref.dtype)

    def far_moves(c):
        at = pl.ds(*scatter[c])
        if SCATTER[c][1]:
            return [remote(far_s.at[at], full_o.at[at], rs_s.at[0, c], rs_r.at[0, c], across, kind="rs")]
        return [
            remote(far_s.at[at, pl.ds(0, half)], half_l.at[at],
                   rs_s.at[0, c], rs_r.at[0, c], right, kind="rs"),
            remote(far_s.at[at, pl.ds(half, half)], half_r.at[at],
                   rs_s.at[1, c], rs_r.at[1, c], left, kind="rs"),
        ]

    def sum_moves(c):
        at = pl.ds(*scatter[c])
        return [
            remote(right_s.at[at], full_l.at[at], rs_s.at[2, c], rs_r.at[2, c], right, kind="rs"),
            remote(left_s.at[at], full_r.at[at], rs_s.at[3, c], rs_r.at[3, c], left, kind="rs"),
        ]

    parts = len(SCATTER)
    far_copies = [far_moves(c) for c in range(parts)]
    sum_copies = [sum_moves(c) for c in range(parts)]

    def add_halves(c):
        at = pl.ds(*scatter[c])
        landed(far_copies[c][:1])
        right_s[at, 0:half] = (right_p[at, 0:half] + half_l[at].astype(F32)).astype(BF16)
        right_s[at, half:] = right_p[at, half:].astype(BF16)
        start(sum_copies[c][:1])
        landed(far_copies[c][1:])
        left_s[at, 0:half] = left_p[at, 0:half].astype(BF16)
        left_s[at, half:] = (left_p[at, half:] + half_r[at].astype(F32)).astype(BF16)
        start(sum_copies[c][1:])

    def finish(c):
        at = pl.ds(*scatter[c])
        landed(sum_copies[c])
        total = full_l[at].astype(F32) + full_r[at].astype(F32)
        if SCATTER[c][1]:
            landed(far_copies[c])
            total = total + full_o[at].astype(F32)
        out_v[at] = (own_p[at] + total).astype(BF16)

    for c in range(parts):
        attend(c)
        output_part(c, 3, far_s)
        start(far_copies[c])
        if c >= 1 and not SCATTER[c - 1][1]:
            add_halves(c - 1)
        if SCATTER[c][1]:
            output_part(c, 1, right_s)
            start(sum_copies[c][:1])
            output_part(c, 2, left_s)
            start(sum_copies[c][1:])
        else:
            output_part(c, 1, right_p)
            output_part(c, 2, left_p)
        output_part(c, 0, own_p)
        if c >= 2:
            finish(c - 2)
    if not SCATTER[-1][1]:
        add_halves(parts - 1)
    finish(parts - 2)
    finish(parts - 1)
    for move in started:
        move.sent()


def body(n_seq, n_tp, hidden_in, doc_lengths, w_query, w_key, w_value, w_out):
    tok, dx = hidden_in.shape
    nq = w_query.shape[1]
    nkv = w_key.shape[1]
    anywhere = pl.BlockSpec(memory_space=pl.ANY)
    dma = pltpu.SemaphoreType.DMA
    count, parts = len(GATHER), len(SCATTER)
    return pl.pallas_call(
        functools.partial(layer, n_seq, n_tp),
        out_shape=pltpu.VMEM((tok, dx), BF16),
        in_specs=[pl.BlockSpec(memory_space=pltpu.SMEM), pl.BlockSpec(memory_space=pltpu.VMEM)]
        + [anywhere] * 5,
        out_specs=pl.BlockSpec(memory_space=pltpu.VMEM),
        scratch_shapes=[
            pltpu.VMEM((tok, 4 * dx), BF16),
            pltpu.VMEM((4 * dx, 2 * nkv + nq), BF16),
            pltpu.VMEM((4, nq, dx), BF16),
            pltpu.VMEM((tok, 2 * nkv), F32),
            pltpu.VMEM((2, 6 * tok + HEAD, 3 * HEAD), BF16),
            pltpu.VMEM((nq // HEAD, tok, HEAD), BF16),
            pltpu.VMEM((4, tok, HEAD), F32),
            pltpu.VMEM((tok, SPAN), F32),
            pltpu.VMEM((tok, nq), BF16),
            pltpu.VMEM((tok, dx), BF16),
            pltpu.VMEM((tok, dx), F32),
            pltpu.VMEM((tok, dx), F32),
            pltpu.VMEM((tok, dx), F32),
            pltpu.VMEM((tok, dx), BF16),
            pltpu.VMEM((tok, dx), BF16),
            pltpu.VMEM((tok, dx // 2), BF16),
            pltpu.VMEM((tok, dx // 2), BF16),
            pltpu.VMEM((tok, dx), BF16),
            pltpu.VMEM((tok, dx), BF16),
            pltpu.VMEM((tok, dx), BF16),
            dma((16,)),
            dma(()),
            dma((2, count)),
            dma((2, count)),
            dma((2, count)),
            dma((2, count)),
            dma((5, count)),
            dma((5, count)),
            dma((4, parts)),
            dma((4, parts)),
        ],
        compiler_params=pltpu.CompilerParams(
            collective_id=0, has_side_effects=True, vmem_limit_bytes=58 * 2**20
        ),
        cost_estimate=pl.CostEstimate(
            flops=7 * 10**9, bytes_accessed=22 * 10**6, transcendentals=2 * 10**6
        ),
        name="layer",
    )(doc_lengths, jnp.asarray(inverse_frequencies()), hidden_in, w_query, w_key, w_value, w_out)


def solution(mesh):
    return jax.shard_map(
        functools.partial(body, mesh.shape["seq"], mesh.shape["tp"]),
        mesh=mesh,
        in_specs=(P("seq", "tp"), P(), P(None, "tp"), P(None, "tp"), P(None, "tp"), P("tp", None)),
        out_specs=P("seq", "tp"),
        check_vma=False,
    )
```

```python
import functools
import math

import jax
import jax.numpy as jnp
import numpy as np
from jax import lax
from jax.experimental import pallas as pl
from jax.experimental.pallas import tpu as pltpu
from jax.sharding import PartitionSpec as P

HEAD = 128
REACH = 4
GATHER = ((64, False, "pass"), (64, False, "pass"), (64, False, "pass"), (64, False, "two"))
SCATTER = ((64, False), (64, False), (64, False), (64, False))
SPAN = 1152
EARLY = 2
MESH = pl.DeviceIdType.MESH
F32 = jnp.float32
BF16 = jnp.bfloat16
OFF = frozenset()


def inverse_frequencies():
    exponent = np.arange(0, HEAD, 2, dtype=np.float32) / np.float32(HEAD)
    base = np.power(np.float32(500000.0), -exponent).astype(np.float32)
    wavelength = (2.0 * math.pi / base).astype(np.float32)
    smooth = (8192.0 / wavelength - 1.0) / 3.0
    blended = (1.0 - smooth) * base / 8.0 + smooth * base
    freq = np.where(wavelength < 2048.0, base, np.where(wavelength > 8192.0, base / 8.0, blended))
    return np.concatenate([freq, freq]).astype(np.float32)[None, :]


def bounds(chunks):
    at, out = 0, []
    for size in chunks:
        out.append((at, size))
        at += size
    return out


class Move:
    def __init__(self, copy, sends=None, lands=None):
        self.copy, self.sends, self.lands = copy, sends, lands

    @staticmethod
    def on(condition, act):
        if condition is None:
            act()
        else:
            pl.when(condition)(act)

    def start(self):
        self.on(self.sends, self.copy.start)

    def sent(self):
        self.on(self.sends, self.copy.wait_send)

    def landed(self):
        self.on(self.lands, self.copy.wait_recv)


class Nothing:
    def start(self):
        pass

    sent = landed = start


def layer(
    n_seq, n_tp,
    len_ref, freq_ref, hid_hbm, wq_hbm, wk_hbm, wv_hbm, wo_hbm, out_v,
    hid, w, wo, acc, kv, q, tab, bias, ctx,
    far_s, right_p, left_p, own_p, right_s, left_s, half_l, half_r, full_l, full_r, full_o,
    w_sem, hid_sem, near_s, near_r, fwd_s, fwd_r, kv_s, kv_r, rs_s, rs_r,
):
    tok, dx = hid_hbm.shape
    docs = len_ref.shape[0]
    nkv = 2 * HEAD
    nq = wq_hbm.shape[1]
    group = nq // HEAD // 2
    half = dx // 2
    seq = lax.axis_index("seq")
    x = lax.axis_index("tp")
    core = lax.rem(seq, 2)
    right = {"tp": lax.rem(x + 1, n_tp)}
    left = {"tp": lax.rem(x + n_tp - 1, n_tp)}
    across = {"tp": lax.rem(x + 2, n_tp)}
    sibling = {"seq": seq + 1 - 2 * core}
    ahead, ahead2, behind, behind2 = ({"seq": seq + d} for d in (2, 4, -2, -4))
    has_ahead, has_ahead2 = seq + 2 < n_seq, seq + 4 < n_seq
    has_behind, has_behind2 = seq >= 2, seq >= 4
    gather = bounds([c[0] for c in GATHER])
    scatter = bounds([c[0] for c in SCATTER])

    @pl.when(seq < 4)
    def _():
        kv[:, 0:4 * tok] = jnp.zeros((2, 4 * tok, 3 * HEAD), BF16)

    @pl.when(core == 0)
    def _():
        kv[:, 5 * tok:6 * tok, 0:nkv] = jnp.zeros((2, tok, nkv), BF16)

    barrier = pltpu.get_barrier_semaphore()

    def greet(other):
        pl.semaphore_signal(barrier, inc=1, device_id=other, device_id_type=MESH)

    for other in (right, left, across, sibling):
        greet(other)
    for other, there in (
        (ahead, has_ahead), (behind, has_behind), (ahead2, has_ahead2), (behind2, has_behind2)
    ):
        pl.when(there)(functools.partial(greet, other))

    shards = (x, lax.rem(x + n_tp - 1, n_tp), lax.rem(x + 1, n_tp), lax.rem(x + 2, n_tp))
    own_copy = pltpu.make_async_copy(hid_hbm, hid.at[:, pl.ds(0, dx)], hid_sem)
    own_copy.start()
    loads = {}

    def load(name, index, src, dst):
        copy = pltpu.make_async_copy(src, dst, w_sem.at[index])
        copy.start()
        loads.setdefault(name, []).append(copy)

    def load_keys(r):
        src = pl.ds(pl.multiple_of(shards[r] * dx, dx), dx)
        dst = pl.ds(r * dx, dx)
        name = "far" if r == 3 else "near"
        load(name, 3 * r, wk_hbm.at[src], w.at[dst, pl.ds(0, nkv)])
        load(name, 3 * r + 1, wv_hbm.at[src], w.at[dst, pl.ds(nkv, nkv)])

    load_keys(0)
    row = lax.broadcasted_iota(jnp.int32, (tok, HEAD), 0)
    lane = lax.broadcasted_iota(jnp.int32, (tok, HEAD), 1)
    pos = row + seq * tok

    def next_doc(d, state):
        end, first = state
        end = end + len_ref[d]
        return end, jnp.where(pos >= end, end, first)

    _, first = lax.fori_loop(0, docs, next_doc, (jnp.int32(0), jnp.zeros_like(pos)))
    angle = (pos - first).astype(F32) * freq_ref[...]
    cosine = jnp.cos(angle)
    sine = jnp.where(lane < HEAD // 2, -1.0, 1.0) * jnp.sin(angle)
    scale = math.log2(math.e) / math.sqrt(HEAD)
    tab[0] = cosine
    tab[1] = sine
    tab[2] = cosine * scale
    tab[3] = sine * scale
    low = first - (seq * tok - REACH * tok)
    high = row + REACH * tok
    for at, size in scatter:
        part = slice(at, at + size)
        for k in range(SPAN // HEAD):
            key = lane[part] + (at + k * HEAD)
            seen = (key >= low[part]) & (key <= high[part])
            bias[part, k * HEAD:(k + 1) * HEAD] = jnp.where(seen, 0.0, -1e30)
    kv[:, :, nkv:] = jnp.ones((2, kv.shape[1], HEAD), BF16)
    kv[:, 6 * tok:, 0:nkv] = jnp.zeros((2, kv.shape[1] - 6 * tok, nkv), BF16)

    others = 4
    for there in (has_ahead, has_behind, has_ahead2, has_behind2):
        others = others + jnp.where(there, 1, 0)
    pl.semaphore_wait(barrier, others)

    def remote(src, dst, send, recv, to, sends=None, lands=None, kind=""):
        if kind in OFF:
            return Nothing()
        copy = pltpu.make_async_remote_copy(
            src_ref=src, dst_ref=dst, send_sem=send, recv_sem=recv,
            device_id=to, device_id_type=MESH,
        )
        return Move(copy, sends, lands)

    def near(c):
        at = pl.ds(*gather[c])
        moves = [
            remote(hid_hbm.at[at], hid.at[at, pl.ds(dx, dx)],
                   near_s.at[0, c], near_r.at[0, c], right, kind="ag"),
            remote(hid_hbm.at[at], hid.at[at, pl.ds(2 * dx, dx)],
                   near_s.at[1, c], near_r.at[1, c], left, kind="ag"),
        ]
        return moves

    def far(c):
        at = pl.ds(*gather[c])
        if GATHER[c][1]:
            return [remote(hid_hbm.at[at], hid.at[at, pl.ds(3 * dx, dx)],
                           fwd_s.at[0, c], fwd_r.at[0, c], across, kind="ag")]
        return [
            remote(hid.at[at, pl.ds(dx, half)], hid.at[at, pl.ds(3 * dx, half)],
                   fwd_s.at[0, c], fwd_r.at[0, c], right, kind="ag"),
            remote(hid.at[at, pl.ds(2 * dx + half, half)],
                   hid.at[at, pl.ds(3 * dx + half, half)],
                   fwd_s.at[1, c], fwd_r.at[1, c], left, kind="ag"),
        ]

    def place(block, c):
        first, size = gather[c]
        return pl.ds(pl.multiple_of((block + core) * tok + first, 16), size)

    def kv_move(kind, c):
        passes = GATHER[c][2] == "pass"
        first_core, second_core = core == 0, core == 1
        src, dst, to, sends, lands = (
            (4, 2, ahead, has_ahead, has_behind),
            (2, 0, ahead, has_ahead & has_behind, has_behind2) if passes
            else (4, 0, ahead2, has_ahead2, has_behind2),
            (4, 4, sibling, first_core, second_core),
            (2, 2, sibling, has_behind, has_behind),
            (0, 0, sibling, has_behind2 & second_core, has_behind2 & first_core),
        )[kind]
        return remote(
            kv.at[:, place(src, c), pl.ds(0, nkv)], kv.at[:, place(dst, c), pl.ds(0, nkv)],
            kv_s.at[kind, c], kv_r.at[kind, c], to, sends, lands, kind="kvx",
        )

    started = []

    def start(moves):
        for move in moves:
            move.start()
            started.append(move)

    def landed(moves):
        for move in moves:
            move.landed()

    count = len(GATHER)
    nears = [near(c) for c in range(count)]
    fars = [far(c) for c in range(count)]
    kvs = [[kv_move(kind, c) for c in range(count)] for kind in range(5)]
    def start_near(c):
        start(nears[c])
        if GATHER[c][1]:
            start(fars[c])

    for c in range(min(EARLY, count)):
        start_near(c)
    for r in (1, 2, 3):
        load_keys(r)
    for r in range(4):
        src = pl.ds(pl.multiple_of(shards[r] * dx, dx), dx)
        load("q", 3 * r + 2, wq_hbm.at[src], w.at[pl.ds(r * dx, dx), pl.ds(2 * nkv, nq)])
    for r, shard in enumerate((shards[0], shards[2], shards[1], shards[3])):
        columns = pl.ds(pl.multiple_of(shard * dx, dx), dx)
        load("out", 12 + r, wo_hbm.at[:, columns], wo.at[r])

    def near_keys(c):
        if "qkv" in OFF:
            return
        at = pl.ds(*gather[c])
        acc[at] = jnp.dot(hid[at, 0:3 * dx], w[0:3 * dx, 0:2 * nkv], preferred_element_type=F32)

    def rotated(part, at, which):
        return part * tab[which, at] + pltpu.roll(part, HEAD // 2, 1) * tab[which + 1, at]

    def far_keys(c):
        at = pl.ds(*gather[c])
        own = place(4, c)
        if "qkv" not in OFF:
            both = acc[at] + jnp.dot(
                hid[at, 3 * dx:], w[3 * dx:, 0:2 * nkv], preferred_element_type=F32
            )
            for g in range(2):
                one = slice(g * HEAD, (g + 1) * HEAD)
                kv[g, own, 0:HEAD] = rotated(both[:, one], at, 0).astype(BF16)
                kv[g, own, HEAD:nkv] = both[:, nkv + g * HEAD:nkv + (g + 1) * HEAD].astype(BF16)
        start([kvs[0][c], kvs[2][c]])
        if GATHER[c][2] == "two":
            start([kvs[1][c]])

    def pass_on(c):
        landed([kvs[0][c]])
        if GATHER[c][2] == "pass":
            start([kvs[1][c]])
        start([kvs[3][c]])

    def pass_far(c):
        landed([kvs[1][c]])
        start([kvs[4][c]])

    def project_queries(j):
        if "qkv" in OFF:
            return
        at = pl.ds(0, tok)
        two = jnp.dot(
            hid[...], w[:, 2 * nkv + 2 * j * HEAD:2 * nkv + 2 * (j + 1) * HEAD],
            preferred_element_type=F32,
        )
        for k in range(2):
            q[2 * j + k] = rotated(two[:, k * HEAD:(k + 1) * HEAD], at, 2).astype(BF16)

    def loaded(name):
        for copy in loads[name]:
            copy.wait()

    own_copy.wait()
    for c in range(count):
        landed(nears[c])
        if not GATHER[c][1]:
            start(fars[c])
        if c + EARLY < count:
            start_near(c + EARLY)
        if c == 0:
            loaded("near")
        near_keys(c)
        if c >= 1:
            if c == 1:
                loaded("far")
            landed(fars[c - 1])
            far_keys(c - 1)
        if c >= 2:
            pass_on(c - 2)
        if c >= 3:
            pass_far(c - 3)
    landed(fars[count - 1])
    far_keys(count - 1)
    loaded("q")
    pass_on(count - 2)
    pass_far(count - 3)
    project_queries(0)
    project_queries(1)
    pass_far(count - 2)
    project_queries(2)
    pass_on(count - 1)
    project_queries(3)
    pass_far(count - 1)
    loaded("out")
    for kind in (2, 3, 4):
        landed(kvs[kind])

    def attend(c):
        if "att" in OFF:
            return
        first, size = scatter[c]
        at = pl.ds(first, size)
        window = pl.ds(pl.multiple_of(core * tok + first, 16), SPAN)
        for g in range(2):
            mine = q[g * group:(g + 1) * group, at].reshape(group * size, HEAD)
            scores = lax.dot_general(
                mine, kv[g, window, 0:HEAD], (((1,), (1,)), ((), ())), preferred_element_type=F32
            )
            scores = scores.reshape(group, size, SPAN) + bias[at][None]
            peak = jnp.max(scores, axis=2, keepdims=True)
            weights = jnp.exp2(scores - peak).reshape(group * size, SPAN).astype(BF16)
            both = jnp.dot(weights, kv[g, window, HEAD:], preferred_element_type=F32)
            value = (both[:, 0:HEAD] / both[:, HEAD:]).astype(BF16)
            for h in range(group):
                to = (g * group + h) * HEAD
                ctx[at, to:to + HEAD] = value[h * size:(h + 1) * size]

    def output_part(c, r, ref):
        if "proj" in OFF:
            return
        at = pl.ds(*scatter[c])
        ref[at] = jnp.dot(ctx[at], wo[r], preferred_element_type=F32).astype(ref.dtype)

    def far_moves(c):
        at = pl.ds(*scatter[c])
        if SCATTER[c][1]:
            return [remote(far_s.at[at], full_o.at[at], rs_s.at[0, c], rs_r.at[0, c], across, kind="rs")]
        return [
            remote(far_s.at[at, pl.ds(0, half)], half_l.at[at],
                   rs_s.at[0, c], rs_r.at[0, c], right, kind="rs"),
            remote(far_s.at[at, pl.ds(half, half)], half_r.at[at],
                   rs_s.at[1, c], rs_r.at[1, c], left, kind="rs"),
        ]

    def sum_moves(c):
        at = pl.ds(*scatter[c])
        return [
            remote(right_s.at[at], full_l.at[at], rs_s.at[2, c], rs_r.at[2, c], right, kind="rs"),
            remote(left_s.at[at], full_r.at[at], rs_s.at[3, c], rs_r.at[3, c], left, kind="rs"),
        ]

    parts = len(SCATTER)
    far_copies = [far_moves(c) for c in range(parts)]
    sum_copies = [sum_moves(c) for c in range(parts)]

    def add_halves(c):
        at = pl.ds(*scatter[c])
        landed(far_copies[c][:1])
        right_s[at, 0:half] = (right_p[at, 0:half] + half_l[at].astype(F32)).astype(BF16)
        right_s[at, half:] = right_p[at, half:].astype(BF16)
        start(sum_copies[c][:1])
        landed(far_copies[c][1:])
        left_s[at, 0:half] = left_p[at, 0:half].astype(BF16)
        left_s[at, half:] = (left_p[at, half:] + half_r[at].astype(F32)).astype(BF16)
        start(sum_copies[c][1:])

    def finish(c):
        at = pl.ds(*scatter[c])
        landed(sum_copies[c])
        total = full_l[at].astype(F32) + full_r[at].astype(F32)
        if SCATTER[c][1]:
            landed(far_copies[c])
            total = total + full_o[at].astype(F32)
        out_v[at] = (own_p[at] + total).astype(BF16)

    for c in range(parts):
        attend(c)
        output_part(c, 3, far_s)
        start(far_copies[c])
        if c >= 1 and not SCATTER[c - 1][1]:
            add_halves(c - 1)
        if SCATTER[c][1]:
            output_part(c, 1, right_s)
            start(sum_copies[c][:1])
            output_part(c, 2, left_s)
            start(sum_copies[c][1:])
        else:
            output_part(c, 1, right_p)
            output_part(c, 2, left_p)
        if c >= 1:
            output_part(c - 1, 0, own_p)
        if c >= 2:
            finish(c - 2)
    if not SCATTER[-1][1]:
        add_halves(parts - 1)
    output_part(parts - 1, 0, own_p)
    finish(parts - 2)
    finish(parts - 1)
    for move in started:
        move.sent()


def body(n_seq, n_tp, hidden_in, doc_lengths, w_query, w_key, w_value, w_out):
    tok, dx = hidden_in.shape
    nq = w_query.shape[1]
    nkv = w_key.shape[1]
    anywhere = pl.BlockSpec(memory_space=pl.ANY)
    dma = pltpu.SemaphoreType.DMA
    count, parts = len(GATHER), len(SCATTER)
    return pl.pallas_call(
        functools.partial(layer, n_seq, n_tp),
        out_shape=pltpu.VMEM((tok, dx), BF16),
        in_specs=[pl.BlockSpec(memory_space=pltpu.SMEM), pl.BlockSpec(memory_space=pltpu.VMEM)]
        + [anywhere] * 5,
        out_specs=pl.BlockSpec(memory_space=pltpu.VMEM),
        scratch_shapes=[
            pltpu.VMEM((tok, 4 * dx), BF16),
            pltpu.VMEM((4 * dx, 2 * nkv + nq), BF16),
            pltpu.VMEM((4, nq, dx), BF16),
            pltpu.VMEM((tok, 2 * nkv), F32),
            pltpu.VMEM((2, 6 * tok + HEAD, 3 * HEAD), BF16),
            pltpu.VMEM((nq // HEAD, tok, HEAD), BF16),
            pltpu.VMEM((4, tok, HEAD), F32),
            pltpu.VMEM((tok, SPAN), F32),
            pltpu.VMEM((tok, nq), BF16),
            pltpu.VMEM((tok, dx), BF16),
            pltpu.VMEM((tok, dx), F32),
            pltpu.VMEM((tok, dx), F32),
            pltpu.VMEM((tok, dx), F32),
            pltpu.VMEM((tok, dx), BF16),
            pltpu.VMEM((tok, dx), BF16),
            pltpu.VMEM((tok, dx // 2), BF16),
            pltpu.VMEM((tok, dx // 2), BF16),
            pltpu.VMEM((tok, dx), BF16),
            pltpu.VMEM((tok, dx), BF16),
            pltpu.VMEM((tok, dx), BF16),
            dma((16,)),
            dma(()),
            dma((2, count)),
            dma((2, count)),
            dma((2, count)),
            dma((2, count)),
            dma((5, count)),
            dma((5, count)),
            dma((4, parts)),
            dma((4, parts)),
        ],
        compiler_params=pltpu.CompilerParams(
            collective_id=0, has_side_effects=True, vmem_limit_bytes=58 * 2**20
        ),
        cost_estimate=pl.CostEstimate(
            flops=7 * 10**9, bytes_accessed=22 * 10**6, transcendentals=2 * 10**6
        ),
        name="layer",
    )(doc_lengths, jnp.asarray(inverse_frequencies()), hidden_in, w_query, w_key, w_value, w_out)


def solution(mesh):
    return jax.shard_map(
        functools.partial(body, mesh.shape["seq"], mesh.shape["tp"]),
        mesh=mesh,
        in_specs=(P("seq", "tp"), P(), P(None, "tp"), P(None, "tp"), P(None, "tp"), P("tp", None)),
        out_specs=P("seq", "tp"),
        check_vma=False,
    )
```

```python
import functools
import math

import jax
import jax.numpy as jnp
import numpy as np
from jax import lax
from jax.experimental import pallas as pl
from jax.experimental.pallas import tpu as pltpu
from jax.sharding import PartitionSpec as P

HEAD = 128
REACH = 4
GATHER = ((32, False, "pass"), (48, False, "pass"), (48, False, "pass"), (48, False, "pass"), (48, False, "pass"), (32, False, "two"))
ORDER = (
    ("send", 0), ("send", 1), ("send", 2), ("send", 3), ("near", 0), ("sum", 0),
    ("near", 1), ("sum", 1), ("near", 2), ("near", 3), ("sum", 3), ("send", 4),
    ("far", 0), ("send", 5), ("far", 1), ("sum", 2), ("far", 2), ("far", 3),
    ("pass", 0), ("near", 4), ("pass", 1), ("sum", 4), ("near", 5), ("pass", 2),
    ("sum", 5), ("pass", 3), ("far", 4), ("share", 0), ("share", 1), ("far", 5),
    ("pass", 4), ("query", 1), ("query", 3), ("share", 2), ("share", 3), ("query", 2),
    ("pass", 5), ("share", 4), ("share", 5), ("query", 0),
)
SCATTER = ((64, False), (64, False), (64, False), (64, False))
SPAN = 1152
MESH = pl.DeviceIdType.MESH
F32 = jnp.float32
BF16 = jnp.bfloat16
OFF = frozenset()


def inverse_frequencies():
    exponent = np.arange(0, HEAD, 2, dtype=np.float32) / np.float32(HEAD)
    base = np.power(np.float32(500000.0), -exponent).astype(np.float32)
    wavelength = (2.0 * math.pi / base).astype(np.float32)
    smooth = (8192.0 / wavelength - 1.0) / 3.0
    blended = (1.0 - smooth) * base / 8.0 + smooth * base
    freq = np.where(wavelength < 2048.0, base, np.where(wavelength > 8192.0, base / 8.0, blended))
    return np.concatenate([freq, freq]).astype(np.float32)[None, :]


def bounds(chunks):
    at, out = 0, []
    for size in chunks:
        out.append((at, size))
        at += size
    return out


class Move:
    def __init__(self, copy, sends=None, lands=None):
        self.copy, self.sends, self.lands = copy, sends, lands

    @staticmethod
    def on(condition, act):
        if condition is None:
            act()
        else:
            pl.when(condition)(act)

    def start(self):
        self.on(self.sends, self.copy.start)

    def sent(self):
        self.on(self.sends, self.copy.wait_send)

    def landed(self):
        self.on(self.lands, self.copy.wait_recv)


class Nothing:
    def start(self):
        pass

    sent = landed = start


def layer(
    n_seq, n_tp,
    len_ref, freq_ref, hid_hbm, wq_hbm, wk_hbm, wv_hbm, wo_hbm, out_v,
    hid, w, wo, acc, kv, q, tab, bias, ctx,
    far_s, right_p, left_p, own_p, right_s, left_s, half_l, half_r, full_l, full_r, full_o,
    w_sem, hid_sem, near_s, near_r, fwd_s, fwd_r, kv_s, kv_r, rs_s, rs_r,
):
    tok, dx = hid_hbm.shape
    docs = len_ref.shape[0]
    nkv = 2 * HEAD
    nq = wq_hbm.shape[1]
    group = nq // HEAD // 2
    half = dx // 2
    seq = lax.axis_index("seq")
    x = lax.axis_index("tp")
    core = lax.rem(seq, 2)
    right = {"tp": lax.rem(x + 1, n_tp)}
    left = {"tp": lax.rem(x + n_tp - 1, n_tp)}
    across = {"tp": lax.rem(x + 2, n_tp)}
    sibling = {"seq": seq + 1 - 2 * core}
    ahead, ahead2, behind, behind2 = ({"seq": seq + d} for d in (2, 4, -2, -4))
    has_ahead, has_ahead2 = seq + 2 < n_seq, seq + 4 < n_seq
    has_behind, has_behind2 = seq >= 2, seq >= 4
    gather = bounds([c[0] for c in GATHER])
    scatter = bounds([c[0] for c in SCATTER])

    @pl.when(seq < 4)
    def _():
        kv[:, 0:4 * tok] = jnp.zeros((2, 4 * tok, 3 * HEAD), BF16)

    @pl.when(core == 0)
    def _():
        kv[:, 5 * tok:6 * tok, 0:nkv] = jnp.zeros((2, tok, nkv), BF16)

    barrier = pltpu.get_barrier_semaphore()

    def greet(other):
        pl.semaphore_signal(barrier, inc=1, device_id=other, device_id_type=MESH)

    for other in (right, left, across, sibling):
        greet(other)
    for other, there in (
        (ahead, has_ahead), (behind, has_behind), (ahead2, has_ahead2), (behind2, has_behind2)
    ):
        pl.when(there)(functools.partial(greet, other))

    shards = (x, lax.rem(x + n_tp - 1, n_tp), lax.rem(x + 1, n_tp), lax.rem(x + 2, n_tp))
    own_copy = pltpu.make_async_copy(hid_hbm, hid.at[:, pl.ds(0, dx)], hid_sem)
    own_copy.start()
    loads = {}

    def load(name, index, src, dst):
        copy = pltpu.make_async_copy(src, dst, w_sem.at[index])
        copy.start()
        loads.setdefault(name, []).append(copy)

    def load_keys(r):
        src = pl.ds(pl.multiple_of(shards[r] * dx, dx), dx)
        dst = pl.ds(r * dx, dx)
        name = "far" if r == 3 else "near"
        load(name, 3 * r, wk_hbm.at[src], w.at[dst, pl.ds(0, nkv)])
        load(name, 3 * r + 1, wv_hbm.at[src], w.at[dst, pl.ds(nkv, nkv)])

    load_keys(0)
    row = lax.broadcasted_iota(jnp.int32, (tok, HEAD), 0)
    lane = lax.broadcasted_iota(jnp.int32, (tok, HEAD), 1)
    pos = row + seq * tok

    def next_doc(d, state):
        end, first = state
        end = end + len_ref[d]
        return end, jnp.where(pos >= end, end, first)

    _, first = lax.fori_loop(0, docs, next_doc, (jnp.int32(0), jnp.zeros_like(pos)))
    angle = (pos - first).astype(F32) * freq_ref[...]
    cosine = jnp.cos(angle)
    sine = jnp.where(lane < HEAD // 2, -1.0, 1.0) * jnp.sin(angle)
    scale = math.log2(math.e) / math.sqrt(HEAD)
    tab[0] = cosine
    tab[1] = sine
    tab[2] = cosine * scale
    tab[3] = sine * scale
    low = first - (seq * tok - REACH * tok)
    high = row + REACH * tok
    for at, size in scatter:
        part = slice(at, at + size)
        for k in range(SPAN // HEAD):
            key = lane[part] + (at + k * HEAD)
            seen = (key >= low[part]) & (key <= high[part])
            bias[part, k * HEAD:(k + 1) * HEAD] = jnp.where(seen, 0.0, -1e30)
    kv[:, :, nkv:] = jnp.ones((2, kv.shape[1], HEAD), BF16)
    kv[:, 6 * tok:, 0:nkv] = jnp.zeros((2, kv.shape[1] - 6 * tok, nkv), BF16)

    others = 4
    for there in (has_ahead, has_behind, has_ahead2, has_behind2):
        others = others + jnp.where(there, 1, 0)
    pl.semaphore_wait(barrier, others)

    def remote(src, dst, send, recv, to, sends=None, lands=None, kind=""):
        if kind in OFF:
            return Nothing()
        copy = pltpu.make_async_remote_copy(
            src_ref=src, dst_ref=dst, send_sem=send, recv_sem=recv,
            device_id=to, device_id_type=MESH,
        )
        return Move(copy, sends, lands)

    def near(c):
        at = pl.ds(*gather[c])
        moves = [
            remote(hid_hbm.at[at], hid.at[at, pl.ds(dx, dx)],
                   near_s.at[0, c], near_r.at[0, c], right, kind="ag"),
            remote(hid_hbm.at[at], hid.at[at, pl.ds(2 * dx, dx)],
                   near_s.at[1, c], near_r.at[1, c], left, kind="ag"),
        ]
        return moves

    def far(c):
        at = pl.ds(*gather[c])
        if GATHER[c][1]:
            return [remote(hid_hbm.at[at], hid.at[at, pl.ds(3 * dx, dx)],
                           fwd_s.at[0, c], fwd_r.at[0, c], across, kind="ag")]
        return [
            remote(hid.at[at, pl.ds(dx, half)], hid.at[at, pl.ds(3 * dx, half)],
                   fwd_s.at[0, c], fwd_r.at[0, c], right, kind="ag"),
            remote(hid.at[at, pl.ds(2 * dx + half, half)],
                   hid.at[at, pl.ds(3 * dx + half, half)],
                   fwd_s.at[1, c], fwd_r.at[1, c], left, kind="ag"),
        ]

    def place(block, c):
        first, size = gather[c]
        return pl.ds(pl.multiple_of((block + core) * tok + first, 16), size)

    def kv_move(kind, c):
        passes = GATHER[c][2] == "pass"
        first_core, second_core = core == 0, core == 1
        src, dst, to, sends, lands = (
            (4, 2, ahead, has_ahead, has_behind),
            (2, 0, ahead, has_ahead & has_behind, has_behind2) if passes
            else (4, 0, ahead2, has_ahead2, has_behind2),
            (4, 4, sibling, first_core, second_core),
            (2, 2, sibling, has_behind, has_behind),
            (0, 0, sibling, has_behind2 & second_core, has_behind2 & first_core),
        )[kind]
        return remote(
            kv.at[:, place(src, c), pl.ds(0, nkv)], kv.at[:, place(dst, c), pl.ds(0, nkv)],
            kv_s.at[kind, c], kv_r.at[kind, c], to, sends, lands, kind="kvx",
        )

    started = []

    def start(moves):
        for move in moves:
            move.start()
            started.append(move)

    def landed(moves):
        for move in moves:
            move.landed()

    count = len(GATHER)
    nears = [near(c) for c in range(count)]
    fars = [far(c) for c in range(count)]
    kvs = [[kv_move(kind, c) for c in range(count)] for kind in range(5)]
    order = list(ORDER)

    def start_near(c):
        start(nears[c])
        if GATHER[c][1]:
            start(fars[c])

    while order and order[0][0] == "send":
        start_near(order.pop(0)[1])
    for r in (1, 2, 3):
        load_keys(r)
    for r in range(4):
        src = pl.ds(pl.multiple_of(shards[r] * dx, dx), dx)
        load("q", 3 * r + 2, wq_hbm.at[src], w.at[pl.ds(r * dx, dx), pl.ds(2 * nkv, nq)])
    for r, shard in enumerate((shards[0], shards[2], shards[1], shards[3])):
        columns = pl.ds(pl.multiple_of(shard * dx, dx), dx)
        load("out", 12 + r, wo_hbm.at[:, columns], wo.at[r])

    def near_keys(c):
        if "qkv" in OFF:
            return
        at = pl.ds(*gather[c])
        acc[at] = jnp.dot(hid[at, 0:3 * dx], w[0:3 * dx, 0:2 * nkv], preferred_element_type=F32)

    def rotated(part, at, which):
        return part * tab[which, at] + pltpu.roll(part, HEAD // 2, 1) * tab[which + 1, at]

    def far_keys(c):
        at = pl.ds(*gather[c])
        own = place(4, c)
        if "qkv" not in OFF:
            both = acc[at] + jnp.dot(
                hid[at, 3 * dx:], w[3 * dx:, 0:2 * nkv], preferred_element_type=F32
            )
            for g in range(2):
                one = slice(g * HEAD, (g + 1) * HEAD)
                kv[g, own, 0:HEAD] = rotated(both[:, one], at, 0).astype(BF16)
                kv[g, own, HEAD:nkv] = both[:, nkv + g * HEAD:nkv + (g + 1) * HEAD].astype(BF16)
        start([kvs[0][c], kvs[2][c]])
        if GATHER[c][2] == "two":
            start([kvs[1][c]])

    def pass_on(c):
        landed([kvs[0][c]])
        if GATHER[c][2] == "pass":
            start([kvs[1][c]])
        start([kvs[3][c]])

    def pass_far(c):
        landed([kvs[1][c]])
        start([kvs[4][c]])

    def project_queries(j):
        if "qkv" in OFF:
            return
        at = pl.ds(0, tok)
        two = jnp.dot(
            hid[...], w[:, 2 * nkv + 2 * j * HEAD:2 * nkv + 2 * (j + 1) * HEAD],
            preferred_element_type=F32,
        )
        for k in range(2):
            q[2 * j + k] = rotated(two[:, k * HEAD:(k + 1) * HEAD], at, 2).astype(BF16)

    def loaded(name):
        for copy in loads[name]:
            copy.wait()

    def wait_near(c):
        landed(nears[c])
        if not GATHER[c][1]:
            start(fars[c])

    def wait_far(c):
        landed(fars[c])
        far_keys(c)

    steps = {
        "send": start_near, "near": wait_near, "sum": near_keys, "far": wait_far,
        "pass": pass_on, "share": pass_far, "query": project_queries,
    }
    needs = {"sum": "near", "far": "far", "query": "q"}
    own_copy.wait()
    for step, index in order:
        if step in needs:
            loaded(needs.pop(step))
        steps[step](index)
    loaded("out")
    for kind in (2, 3, 4):
        landed(kvs[kind])

    def attend(c):
        if "att" in OFF:
            return
        first, size = scatter[c]
        at = pl.ds(first, size)
        window = pl.ds(pl.multiple_of(core * tok + first, 16), SPAN)
        for g in range(2):
            mine = q[g * group:(g + 1) * group, at].reshape(group * size, HEAD)
            scores = lax.dot_general(
                mine, kv[g, window, 0:HEAD], (((1,), (1,)), ((), ())), preferred_element_type=F32
            )
            scores = scores.reshape(group, size, SPAN) + bias[at][None]
            peak = jnp.max(scores, axis=2, keepdims=True)
            weights = jnp.exp2(scores - peak).reshape(group * size, SPAN).astype(BF16)
            both = jnp.dot(weights, kv[g, window, HEAD:], preferred_element_type=F32)
            value = (both[:, 0:HEAD] / both[:, HEAD:]).astype(BF16)
            for h in range(group):
                to = (g * group + h) * HEAD
                ctx[at, to:to + HEAD] = value[h * size:(h + 1) * size]

    def output_part(c, r, ref):
        if "proj" in OFF:
            return
        at = pl.ds(*scatter[c])
        ref[at] = jnp.dot(ctx[at], wo[r], preferred_element_type=F32).astype(ref.dtype)

    def far_moves(c):
        at = pl.ds(*scatter[c])
        if SCATTER[c][1]:
            return [remote(far_s.at[at], full_o.at[at], rs_s.at[0, c], rs_r.at[0, c], across, kind="rs")]
        return [
            remote(far_s.at[at, pl.ds(0, half)], half_l.at[at],
                   rs_s.at[0, c], rs_r.at[0, c], right, kind="rs"),
            remote(far_s.at[at, pl.ds(half, half)], half_r.at[at],
                   rs_s.at[1, c], rs_r.at[1, c], left, kind="rs"),
        ]

    def sum_moves(c):
        at = pl.ds(*scatter[c])
        return [
            remote(right_s.at[at], full_l.at[at], rs_s.at[2, c], rs_r.at[2, c], right, kind="rs"),
            remote(left_s.at[at], full_r.at[at], rs_s.at[3, c], rs_r.at[3, c], left, kind="rs"),
        ]

    parts = len(SCATTER)
    far_copies = [far_moves(c) for c in range(parts)]
    sum_copies = [sum_moves(c) for c in range(parts)]

    def add_halves(c):
        at = pl.ds(*scatter[c])
        landed(far_copies[c][:1])
        right_s[at, 0:half] = (right_p[at, 0:half] + half_l[at].astype(F32)).astype(BF16)
        right_s[at, half:] = right_p[at, half:].astype(BF16)
        start(sum_copies[c][:1])
        landed(far_copies[c][1:])
        left_s[at, 0:half] = left_p[at, 0:half].astype(BF16)
        left_s[at, half:] = (left_p[at, half:] + half_r[at].astype(F32)).astype(BF16)
        start(sum_copies[c][1:])

    def finish(c):
        at = pl.ds(*scatter[c])
        landed(sum_copies[c])
        total = full_l[at].astype(F32) + full_r[at].astype(F32)
        if SCATTER[c][1]:
            landed(far_copies[c])
            total = total + full_o[at].astype(F32)
        out_v[at] = (own_p[at] + total).astype(BF16)

    for c in range(parts):
        attend(c)
        output_part(c, 3, far_s)
        start(far_copies[c])
        if c >= 1 and not SCATTER[c - 1][1]:
            add_halves(c - 1)
        if SCATTER[c][1]:
            output_part(c, 1, right_s)
            start(sum_copies[c][:1])
            output_part(c, 2, left_s)
            start(sum_copies[c][1:])
        else:
            output_part(c, 1, right_p)
            output_part(c, 2, left_p)
        if c >= 1:
            output_part(c - 1, 0, own_p)
        if c >= 2:
            finish(c - 2)
    if not SCATTER[-1][1]:
        add_halves(parts - 1)
    output_part(parts - 1, 0, own_p)
    finish(parts - 2)
    finish(parts - 1)
    for move in started:
        move.sent()


def body(n_seq, n_tp, hidden_in, doc_lengths, w_query, w_key, w_value, w_out):
    tok, dx = hidden_in.shape
    nq = w_query.shape[1]
    nkv = w_key.shape[1]
    anywhere = pl.BlockSpec(memory_space=pl.ANY)
    dma = pltpu.SemaphoreType.DMA
    count, parts = len(GATHER), len(SCATTER)
    return pl.pallas_call(
        functools.partial(layer, n_seq, n_tp),
        out_shape=pltpu.VMEM((tok, dx), BF16),
        in_specs=[pl.BlockSpec(memory_space=pltpu.SMEM), pl.BlockSpec(memory_space=pltpu.VMEM)]
        + [anywhere] * 5,
        out_specs=pl.BlockSpec(memory_space=pltpu.VMEM),
        scratch_shapes=[
            pltpu.VMEM((tok, 4 * dx), BF16),
            pltpu.VMEM((4 * dx, 2 * nkv + nq), BF16),
            pltpu.VMEM((4, nq, dx), BF16),
            pltpu.VMEM((tok, 2 * nkv), F32),
            pltpu.VMEM((2, 6 * tok + HEAD, 3 * HEAD), BF16),
            pltpu.VMEM((nq // HEAD, tok, HEAD), BF16),
            pltpu.VMEM((4, tok, HEAD), F32),
            pltpu.VMEM((tok, SPAN), F32),
            pltpu.VMEM((tok, nq), BF16),
            pltpu.VMEM((tok, dx), BF16),
            pltpu.VMEM((tok, dx), F32),
            pltpu.VMEM((tok, dx), F32),
            pltpu.VMEM((tok, dx), F32),
            pltpu.VMEM((tok, dx), BF16),
            pltpu.VMEM((tok, dx), BF16),
            pltpu.VMEM((tok, dx // 2), BF16),
            pltpu.VMEM((tok, dx // 2), BF16),
            pltpu.VMEM((tok, dx), BF16),
            pltpu.VMEM((tok, dx), BF16),
            pltpu.VMEM((tok, dx), BF16),
            dma((16,)),
            dma(()),
            dma((2, count)),
            dma((2, count)),
            dma((2, count)),
            dma((2, count)),
            dma((5, count)),
            dma((5, count)),
            dma((4, parts)),
            dma((4, parts)),
        ],
        compiler_params=pltpu.CompilerParams(
            collective_id=0, has_side_effects=True, vmem_limit_bytes=58 * 2**20
        ),
        cost_estimate=pl.CostEstimate(
            flops=7 * 10**9, bytes_accessed=22 * 10**6, transcendentals=2 * 10**6
        ),
        name="layer",
    )(doc_lengths, jnp.asarray(inverse_frequencies()), hidden_in, w_query, w_key, w_value, w_out)


def solution(mesh):
    return jax.shard_map(
        functools.partial(body, mesh.shape["seq"], mesh.shape["tp"]),
        mesh=mesh,
        in_specs=(P("seq", "tp"), P(), P(None, "tp"), P(None, "tp"), P(None, "tp"), P("tp", None)),
        out_specs=P("seq", "tp"),
        check_vma=False,
    )
```

```python
import functools
import math

import jax
import jax.numpy as jnp
import numpy as np
from jax import lax
from jax.experimental import pallas as pl
from jax.experimental.pallas import tpu as pltpu
from jax.sharding import PartitionSpec as P

HEAD = 128
REACH = 4
GATHER = ((32, False, "pass"), (48, False, "pass"), (48, False, "pass"), (48, False, "pass"), (48, False, "pass"), (32, False, "two"))
ORDER = (
    ("send", 0), ("send", 1), ("send", 2), ("send", 3), ("near", 0), ("sum", 0),
    ("near", 1), ("sum", 1), ("near", 2), ("near", 3), ("sum", 3), ("send", 4),
    ("far", 0), ("send", 5), ("far", 1), ("sum", 2), ("far", 2), ("far", 3),
    ("pass", 0), ("near", 4), ("pass", 1), ("sum", 4), ("near", 5), ("pass", 2),
    ("sum", 5), ("pass", 3), ("far", 4), ("share", 0), ("share", 1), ("far", 5),
    ("pass", 4), ("query", 1), ("query", 3), ("share", 2), ("share", 3), ("query", 2),
    ("pass", 5), ("share", 4), ("share", 5), ("query", 0),
)
SCATTER = ((64, False), (80, False), (64, False), (48, False))
SCATTER_ORDER = (
    ("attend", 2), ("far", 2), ("attend", 1), ("far", 1), ("attend", 0), ("far", 0),
    ("left", 2), ("right", 2), ("add", 2), ("right", 1), ("attend", 3), ("right", 3),
    ("far", 3), ("left", 0), ("right", 0), ("add", 0), ("own", 3), ("own", 2),
    ("left", 1), ("left", 3), ("add", 1), ("finish", 2), ("own", 1), ("own", 0),
    ("finish", 0), ("add", 3), ("finish", 1), ("finish", 3),
)
SPAN = 1152
MESH = pl.DeviceIdType.MESH
F32 = jnp.float32
BF16 = jnp.bfloat16
OFF = frozenset()


def inverse_frequencies():
    exponent = np.arange(0, HEAD, 2, dtype=np.float32) / np.float32(HEAD)
    base = np.power(np.float32(500000.0), -exponent).astype(np.float32)
    wavelength = (2.0 * math.pi / base).astype(np.float32)
    smooth = (8192.0 / wavelength - 1.0) / 3.0
    blended = (1.0 - smooth) * base / 8.0 + smooth * base
    freq = np.where(wavelength < 2048.0, base, np.where(wavelength > 8192.0, base / 8.0, blended))
    return np.concatenate([freq, freq]).astype(np.float32)[None, :]


def bounds(chunks):
    at, out = 0, []
    for size in chunks:
        out.append((at, size))
        at += size
    return out


class Move:
    def __init__(self, copy, sends=None, lands=None):
        self.copy, self.sends, self.lands = copy, sends, lands

    @staticmethod
    def on(condition, act):
        if condition is None:
            act()
        else:
            pl.when(condition)(act)

    def start(self):
        self.on(self.sends, self.copy.start)

    def sent(self):
        self.on(self.sends, self.copy.wait_send)

    def landed(self):
        self.on(self.lands, self.copy.wait_recv)


class Nothing:
    def start(self):
        pass

    sent = landed = start


def layer(
    n_seq, n_tp,
    len_ref, freq_ref, hid_hbm, wq_hbm, wk_hbm, wv_hbm, wo_hbm, out_v,
    hid, w, wo, acc, kv, q, tab, bias, ctx,
    far_s, right_p, left_p, own_p, right_s, left_s, half_l, half_r, full_l, full_r, full_o,
    w_sem, hid_sem, near_s, near_r, fwd_s, fwd_r, kv_s, kv_r, rs_s, rs_r,
):
    tok, dx = hid_hbm.shape
    docs = len_ref.shape[0]
    nkv = 2 * HEAD
    nq = wq_hbm.shape[1]
    group = nq // HEAD // 2
    half = dx // 2
    seq = lax.axis_index("seq")
    x = lax.axis_index("tp")
    core = lax.rem(seq, 2)
    right = {"tp": lax.rem(x + 1, n_tp)}
    left = {"tp": lax.rem(x + n_tp - 1, n_tp)}
    across = {"tp": lax.rem(x + 2, n_tp)}
    sibling = {"seq": seq + 1 - 2 * core}
    ahead, ahead2, behind, behind2 = ({"seq": seq + d} for d in (2, 4, -2, -4))
    has_ahead, has_ahead2 = seq + 2 < n_seq, seq + 4 < n_seq
    has_behind, has_behind2 = seq >= 2, seq >= 4
    gather = bounds([c[0] for c in GATHER])
    scatter = bounds([c[0] for c in SCATTER])

    @pl.when(seq < 4)
    def _():
        kv[:, 0:4 * tok] = jnp.zeros((2, 4 * tok, 3 * HEAD), BF16)

    @pl.when(core == 0)
    def _():
        kv[:, 5 * tok:6 * tok, 0:nkv] = jnp.zeros((2, tok, nkv), BF16)

    barrier = pltpu.get_barrier_semaphore()

    def greet(other):
        pl.semaphore_signal(barrier, inc=1, device_id=other, device_id_type=MESH)

    straight = any(c[1] for c in GATHER + SCATTER)
    ring = (right, left, sibling) + ((across,) if straight else ())
    for other in ring:
        greet(other)
    for other, there in (
        (ahead, has_ahead), (behind, has_behind), (ahead2, has_ahead2), (behind2, has_behind2)
    ):
        pl.when(there)(functools.partial(greet, other))

    shards = (x, lax.rem(x + n_tp - 1, n_tp), lax.rem(x + 1, n_tp), lax.rem(x + 2, n_tp))
    own_copy = pltpu.make_async_copy(hid_hbm, hid.at[:, pl.ds(0, dx)], hid_sem)
    own_copy.start()
    loads = {}

    def load(name, index, src, dst):
        copy = pltpu.make_async_copy(src, dst, w_sem.at[index])
        copy.start()
        loads.setdefault(name, []).append(copy)

    def load_keys(r):
        src = pl.ds(pl.multiple_of(shards[r] * dx, dx), dx)
        dst = pl.ds(r * dx, dx)
        name = "far" if r == 3 else "near"
        load(name, 3 * r, wk_hbm.at[src], w.at[dst, pl.ds(0, nkv)])
        load(name, 3 * r + 1, wv_hbm.at[src], w.at[dst, pl.ds(nkv, nkv)])

    load_keys(0)
    row = lax.broadcasted_iota(jnp.int32, (tok, HEAD), 0)
    lane = lax.broadcasted_iota(jnp.int32, (tok, HEAD), 1)
    pos = row + seq * tok

    def next_doc(d, state):
        end, first = state
        end = end + len_ref[d]
        return end, jnp.where(pos >= end, end, first)

    _, first = lax.fori_loop(0, docs, next_doc, (jnp.int32(0), jnp.zeros_like(pos)))
    angle = (pos - first).astype(F32) * freq_ref[...]
    cosine = jnp.cos(angle)
    sine = jnp.where(lane < HEAD // 2, -1.0, 1.0) * jnp.sin(angle)
    scale = math.log2(math.e) / math.sqrt(HEAD)
    tab[0] = cosine
    tab[1] = sine
    tab[2] = cosine * scale
    tab[3] = sine * scale
    low = first - (seq * tok - REACH * tok)
    high = row + REACH * tok
    for at, size in scatter:
        part = slice(at, at + size)
        for k in range(SPAN // HEAD):
            key = lane[part] + (at + k * HEAD)
            seen = (key >= low[part]) & (key <= high[part])
            bias[part, k * HEAD:(k + 1) * HEAD] = jnp.where(seen, 0.0, -1e30)
    kv[:, :, nkv:] = jnp.ones((2, kv.shape[1], HEAD), BF16)
    kv[:, 6 * tok:, 0:nkv] = jnp.zeros((2, kv.shape[1] - 6 * tok, nkv), BF16)

    others = len(ring)
    for there in (has_ahead, has_behind, has_ahead2, has_behind2):
        others = others + jnp.where(there, 1, 0)
    pl.semaphore_wait(barrier, others)

    def remote(src, dst, send, recv, to, sends=None, lands=None, kind=""):
        if kind in OFF:
            return Nothing()
        copy = pltpu.make_async_remote_copy(
            src_ref=src, dst_ref=dst, send_sem=send, recv_sem=recv,
            device_id=to, device_id_type=MESH,
        )
        return Move(copy, sends, lands)

    def near(c):
        at = pl.ds(*gather[c])
        moves = [
            remote(hid_hbm.at[at], hid.at[at, pl.ds(dx, dx)],
                   near_s.at[0, c], near_r.at[0, c], right, kind="ag"),
            remote(hid_hbm.at[at], hid.at[at, pl.ds(2 * dx, dx)],
                   near_s.at[1, c], near_r.at[1, c], left, kind="ag"),
        ]
        return moves

    def far(c):
        at = pl.ds(*gather[c])
        if GATHER[c][1]:
            return [remote(hid_hbm.at[at], hid.at[at, pl.ds(3 * dx, dx)],
                           fwd_s.at[0, c], fwd_r.at[0, c], across, kind="ag")]
        return [
            remote(hid.at[at, pl.ds(dx, half)], hid.at[at, pl.ds(3 * dx, half)],
                   fwd_s.at[0, c], fwd_r.at[0, c], right, kind="ag"),
            remote(hid.at[at, pl.ds(2 * dx + half, half)],
                   hid.at[at, pl.ds(3 * dx + half, half)],
                   fwd_s.at[1, c], fwd_r.at[1, c], left, kind="ag"),
        ]

    def place(block, c):
        first, size = gather[c]
        return pl.ds(pl.multiple_of((block + core) * tok + first, 16), size)

    def kv_move(kind, c):
        passes = GATHER[c][2] == "pass"
        first_core, second_core = core == 0, core == 1
        src, dst, to, sends, lands = (
            (4, 2, ahead, has_ahead, has_behind),
            (2, 0, ahead, has_ahead & has_behind, has_behind2) if passes
            else (4, 0, ahead2, has_ahead2, has_behind2),
            (4, 4, sibling, first_core, second_core),
            (2, 2, sibling, has_behind, has_behind),
            (0, 0, sibling, has_behind2 & second_core, has_behind2 & first_core),
        )[kind]
        return remote(
            kv.at[:, place(src, c), pl.ds(0, nkv)], kv.at[:, place(dst, c), pl.ds(0, nkv)],
            kv_s.at[kind, c], kv_r.at[kind, c], to, sends, lands, kind="kvx",
        )

    started = []

    def start(moves):
        for move in moves:
            move.start()
            started.append(move)

    def landed(moves):
        for move in moves:
            move.landed()

    count = len(GATHER)
    nears = [near(c) for c in range(count)]
    fars = [far(c) for c in range(count)]
    kvs = [[kv_move(kind, c) for c in range(count)] for kind in range(5)]
    order = list(ORDER)

    def start_near(c):
        start(nears[c])
        if GATHER[c][1]:
            start(fars[c])

    while order and order[0][0] == "send":
        start_near(order.pop(0)[1])
    for r in (1, 2, 3):
        load_keys(r)
    for r in range(4):
        src = pl.ds(pl.multiple_of(shards[r] * dx, dx), dx)
        load("q", 3 * r + 2, wq_hbm.at[src], w.at[pl.ds(r * dx, dx), pl.ds(2 * nkv, nq)])
    for r, shard in enumerate((shards[0], shards[2], shards[1], shards[3])):
        columns = pl.ds(pl.multiple_of(shard * dx, dx), dx)
        load("out", 12 + r, wo_hbm.at[:, columns], wo.at[r])

    def near_keys(c):
        if "qkv" in OFF:
            return
        at = pl.ds(*gather[c])
        acc[at] = jnp.dot(hid[at, 0:3 * dx], w[0:3 * dx, 0:2 * nkv], preferred_element_type=F32)

    def rotated(part, at, which):
        return part * tab[which, at] + pltpu.roll(part, HEAD // 2, 1) * tab[which + 1, at]

    def far_keys(c):
        at = pl.ds(*gather[c])
        own = place(4, c)
        if "qkv" not in OFF:
            both = acc[at] + jnp.dot(
                hid[at, 3 * dx:], w[3 * dx:, 0:2 * nkv], preferred_element_type=F32
            )
            for g in range(2):
                one = slice(g * HEAD, (g + 1) * HEAD)
                kv[g, own, 0:HEAD] = rotated(both[:, one], at, 0).astype(BF16)
                kv[g, own, HEAD:nkv] = both[:, nkv + g * HEAD:nkv + (g + 1) * HEAD].astype(BF16)
        start([kvs[0][c], kvs[2][c]])
        if GATHER[c][2] == "two":
            start([kvs[1][c]])

    def pass_on(c):
        landed([kvs[0][c]])
        if GATHER[c][2] == "pass":
            start([kvs[1][c]])
        start([kvs[3][c]])

    def pass_far(c):
        landed([kvs[1][c]])
        start([kvs[4][c]])

    def project_queries(j):
        if "qkv" in OFF:
            return
        at = pl.ds(0, tok)
        two = jnp.dot(
            hid[...], w[:, 2 * nkv + 2 * j * HEAD:2 * nkv + 2 * (j + 1) * HEAD],
            preferred_element_type=F32,
        )
        for k in range(2):
            q[2 * j + k] = rotated(two[:, k * HEAD:(k + 1) * HEAD], at, 2).astype(BF16)

    def loaded(name):
        for copy in loads[name]:
            copy.wait()

    def wait_near(c):
        landed(nears[c])
        if not GATHER[c][1]:
            start(fars[c])

    def wait_far(c):
        landed(fars[c])
        far_keys(c)

    def settle(early):
        for kind, late in ((2, 1), (3, 2), (4, 3)):
            landed(kvs[kind][:count - late] if early else kvs[kind][count - late:])

    steps = {
        "send": start_near, "near": wait_near, "sum": near_keys, "far": wait_far,
        "pass": pass_on, "share": pass_far, "query": project_queries,
    }
    needs = {"sum": "near", "far": "far", "query": "q"}
    own_copy.wait()
    for step, index in order:
        if step in needs:
            loaded(needs.pop(step))
        if (step, index) == ("pass", count - 1):
            settle(True)
        steps[step](index)
    loaded("out")
    settle(False)

    def attend(c):
        if "att" in OFF:
            return
        first, size = scatter[c]
        at = pl.ds(first, size)
        window = pl.ds(pl.multiple_of(core * tok + first, 16), SPAN)
        for g in range(2):
            mine = q[g * group:(g + 1) * group, at].reshape(group * size, HEAD)
            scores = lax.dot_general(
                mine, kv[g, window, 0:HEAD], (((1,), (1,)), ((), ())), preferred_element_type=F32
            )
            scores = scores.reshape(group, size, SPAN) + bias[at][None]
            peak = jnp.max(scores, axis=2, keepdims=True)
            weights = jnp.exp2(scores - peak).reshape(group * size, SPAN).astype(BF16)
            both = jnp.dot(weights, kv[g, window, HEAD:], preferred_element_type=F32)
            value = (both[:, 0:HEAD] / both[:, HEAD:]).astype(BF16)
            for h in range(group):
                to = (g * group + h) * HEAD
                ctx[at, to:to + HEAD] = value[h * size:(h + 1) * size]

    def output_part(c, r, ref):
        if "proj" in OFF:
            return
        at = pl.ds(*scatter[c])
        ref[at] = jnp.dot(ctx[at], wo[r], preferred_element_type=F32).astype(ref.dtype)

    def far_moves(c):
        at = pl.ds(*scatter[c])
        if SCATTER[c][1]:
            return [remote(far_s.at[at], full_o.at[at], rs_s.at[0, c], rs_r.at[0, c], across, kind="rs")]
        return [
            remote(far_s.at[at, pl.ds(0, half)], half_l.at[at],
                   rs_s.at[0, c], rs_r.at[0, c], right, kind="rs"),
            remote(far_s.at[at, pl.ds(half, half)], half_r.at[at],
                   rs_s.at[1, c], rs_r.at[1, c], left, kind="rs"),
        ]

    def sum_moves(c):
        at = pl.ds(*scatter[c])
        return [
            remote(right_s.at[at], full_l.at[at], rs_s.at[2, c], rs_r.at[2, c], right, kind="rs"),
            remote(left_s.at[at], full_r.at[at], rs_s.at[3, c], rs_r.at[3, c], left, kind="rs"),
        ]

    parts = len(SCATTER)
    far_copies = [far_moves(c) for c in range(parts)]
    sum_copies = [sum_moves(c) for c in range(parts)]

    def add_halves(c):
        at = pl.ds(*scatter[c])
        landed(far_copies[c][:1])
        right_s[at, 0:half] = (right_p[at, 0:half] + half_l[at].astype(F32)).astype(BF16)
        right_s[at, half:] = right_p[at, half:].astype(BF16)
        start(sum_copies[c][:1])
        landed(far_copies[c][1:])
        left_s[at, 0:half] = left_p[at, 0:half].astype(BF16)
        left_s[at, half:] = (left_p[at, half:] + half_r[at].astype(F32)).astype(BF16)
        start(sum_copies[c][1:])

    def finish(c):
        at = pl.ds(*scatter[c])
        landed(sum_copies[c])
        total = full_l[at].astype(F32) + full_r[at].astype(F32)
        if SCATTER[c][1]:
            landed(far_copies[c])
            total = total + full_o[at].astype(F32)
        out_v[at] = (own_p[at] + total).astype(BF16)

    def send_far(c):
        output_part(c, 3, far_s)
        start(far_copies[c])

    def toward(side):
        def act(c):
            straight = SCATTER[c][1]
            ref = ((right_p, left_p), (right_s, left_s))[straight][side]
            output_part(c, 1 + side, ref)
            if straight:
                start(sum_copies[c][side:side + 1])
        return act

    steps = {
        "attend": attend, "far": send_far, "right": toward(0), "left": toward(1),
        "own": lambda c: output_part(c, 0, own_p), "add": add_halves, "finish": finish,
    }
    for step, index in SCATTER_ORDER[:-1]:
        steps[step](index)
    for move in started:
        move.sent()
    steps[SCATTER_ORDER[-1][0]](SCATTER_ORDER[-1][1])


def body(n_seq, n_tp, hidden_in, doc_lengths, w_query, w_key, w_value, w_out):
    tok, dx = hidden_in.shape
    nq = w_query.shape[1]
    nkv = w_key.shape[1]
    anywhere = pl.BlockSpec(memory_space=pl.ANY)
    dma = pltpu.SemaphoreType.DMA
    count, parts = len(GATHER), len(SCATTER)
    return pl.pallas_call(
        functools.partial(layer, n_seq, n_tp),
        out_shape=pltpu.VMEM((tok, dx), BF16),
        in_specs=[pl.BlockSpec(memory_space=pltpu.SMEM), pl.BlockSpec(memory_space=pltpu.VMEM)]
        + [anywhere] * 5,
        out_specs=pl.BlockSpec(memory_space=pltpu.VMEM),
        scratch_shapes=[
            pltpu.VMEM((tok, 4 * dx), BF16),
            pltpu.VMEM((4 * dx, 2 * nkv + nq), BF16),
            pltpu.VMEM((4, nq, dx), BF16),
            pltpu.VMEM((tok, 2 * nkv), F32),
            pltpu.VMEM((2, 6 * tok + HEAD, 3 * HEAD), BF16),
            pltpu.VMEM((nq // HEAD, tok, HEAD), BF16),
            pltpu.VMEM((4, tok, HEAD), F32),
            pltpu.VMEM((tok, SPAN), F32),
            pltpu.VMEM((tok, nq), BF16),
            pltpu.VMEM((tok, dx), BF16),
            pltpu.VMEM((tok, dx), F32),
            pltpu.VMEM((tok, dx), F32),
            pltpu.VMEM((tok, dx), F32),
            pltpu.VMEM((tok, dx), BF16),
            pltpu.VMEM((tok, dx), BF16),
            pltpu.VMEM((tok, dx // 2), BF16),
            pltpu.VMEM((tok, dx // 2), BF16),
            pltpu.VMEM((tok, dx), BF16),
            pltpu.VMEM((tok, dx), BF16),
            pltpu.VMEM((tok, dx), BF16),
            dma((16,)),
            dma(()),
            dma((2, count)),
            dma((2, count)),
            dma((2, count)),
            dma((2, count)),
            dma((5, count)),
            dma((5, count)),
            dma((4, parts)),
            dma((4, parts)),
        ],
        compiler_params=pltpu.CompilerParams(
            collective_id=0, has_side_effects=True, vmem_limit_bytes=58 * 2**20
        ),
        cost_estimate=pl.CostEstimate(
            flops=7 * 10**9, bytes_accessed=22 * 10**6, transcendentals=2 * 10**6
        ),
        name="layer",
    )(doc_lengths, jnp.asarray(inverse_frequencies()), hidden_in, w_query, w_key, w_value, w_out)


def solution(mesh):
    return jax.shard_map(
        functools.partial(body, mesh.shape["seq"], mesh.shape["tp"]),
        mesh=mesh,
        in_specs=(P("seq", "tp"), P(), P(None, "tp"), P(None, "tp"), P(None, "tp"), P("tp", None)),
        out_specs=P("seq", "tp"),
        check_vma=False,
    )
```
